256 devices in a mesh: rep: 8 (over z_hi, y), fsdp: 32 (over z_lo, x, core).
Axes of the slice: x: 4, y: 4, z: 8 (z_hi: 2, z_lo: 4; z = z_hi * 4 + z_lo), core: 2. Of those that a mesh axis runs over, the one named last changes fastest.
Arguments:
- acts: bfloat16 [8, 8192, 7168], P('rep', 'fsdp'), may hold values from -6 to 6
- key_weight: bfloat16 [8, 7168, 512], P('rep', 'fsdp'), may hold values from -0.0625 to 0.0625
- cotangent: bfloat16 [8, 8192, 512], P('rep', 'fsdp'), may hold values from -6 to 6
- frag_local: bfloat16 [8, 7168, 1024], P('rep', 'fsdp'), may hold values from -6 to 6
- frag_anchor: float32 [7168, 1024], P('fsdp', 'rep'), may hold values from -6 to 6
- frag_moment: float32 [7168, 1024], P('fsdp', 'rep'), may hold values from -6 to 6
- frag_pending: float32 [7168, 1024], P('fsdp', 'rep'), may hold values from -6 to 6
Outputs:
- keys: bfloat16 [8, 8192, 512], P('rep', 'fsdp')
- key_grad: bfloat16 [8, 7168, 512], P('rep', 'fsdp')
- act_grad: bfloat16 [8, 8192, 7168], P('rep', 'fsdp')
- local_next: bfloat16 [8, 7168, 1024], P('rep', 'fsdp')
- anchor_next: float32 [7168, 1024], P('fsdp', 'rep')
- moment_next: float32 [7168, 1024], P('fsdp', 'rep')
- pending_next: float32 [7168, 1024], P('fsdp', 'rep')
The draws below stay inside these ranges and needn't reach their ends.
All inputs are finite; a program needn't handle non-finite values.
Results may differ from the reference program's by a relative error of at most 0.012.
Values may be sent and summed in bfloat16 or wider, within the bound.
A program may use at most 128 MiB of HBM per device.

```python
import jax
import jax.numpy as jnp
from jax import lax

D = 7168
KW = 512
FW = 1024
REPS = 8
TOKENS_REP = 8192


def with_spikes(drawn, rng, source, target, parts, factor):
    owner, partner = [(jnp.arange(drawn.shape[axis_at]) // (drawn.shape[axis_at] // parts)).reshape([-1 if axis == axis_at else 1 for axis in range(drawn.ndim)]) for axis_at in (source, target)]
    chosen = jax.random.permutation(rng, parts)[partner]
    strong = (owner == chosen) | (owner == (partner + parts // 2) % parts)
    return jnp.where(strong, factor * drawn, drawn)


def shard_levels(rng, shape, cuts, smallest, top_value):
    def one(position, parts):
        heights = jax.random.uniform(jax.random.fold_in(jax.random.fold_in(rng, 6), position), (parts,), jnp.float32, smallest / len(cuts), top_value / len(cuts))
        return jnp.repeat(jnp.exp(heights), shape[position] // parts).reshape((-1,) + (1,) * (len(shape) - position - 1))

    loudness = one(*cuts[0])
    for cut in cuts[1:]:
        loudness = loudness * one(*cut)
    return loudness


def bell_draw(key, extent, scale, reach, shards=(), kind=jnp.bfloat16):
    gain = shard_levels(key, extent, shards, -0.22, 0.18) if shards else 1.0
    values = jax.random.normal(key, extent, jnp.float32) * scale * gain
    return jnp.minimum(jnp.maximum(values, -reach), reach).astype(kind)


def noise_with(key, shape, scale, bound, split, heavy, held_as=jnp.bfloat16):
    drawn = scale * jax.random.normal(key, shape, jnp.float32)
    if split:
        drawn = drawn * shard_levels(key, shape, split, -0.22, 0.18)
    return jnp.clip(with_spikes(drawn, jax.random.fold_in(key, 3), *heavy), -bound, bound).astype(held_as)


def setup_inputs(seed: int = 0) -> dict:
    splits = jax.random.split(jax.random.key(seed), 8)
    return {
        "acts": noise_with(splits[0], (REPS, TOKENS_REP, D), 1.0, 6.0, ((0, 8), (1, 32)), (1, 2, 32, 2.75)),
        "key_weight": bell_draw(splits[1], (REPS, D, KW), D ** -0.5, 0.0625, ((0, 8), (1, 32))),
        "cotangent": bell_draw(splits[2], (REPS, TOKENS_REP, KW), 1.0, 6.0, ((0, 8), (1, 32))),
        "frag_local": bell_draw(splits[3], (REPS, D, FW), 1.0, 6.0, ((0, 8), (1, 32))),
        "frag_anchor": bell_draw(splits[4], (D, FW), 1.0, 6.0, ((0, 32), (1, 8)), jnp.float32),
        "frag_moment": bell_draw(splits[5], (D, FW), 1.0, 6.0, ((0, 32), (1, 8)), jnp.float32),
        "frag_pending": bell_draw(splits[6], (D, FW), 1.0, 6.0, ((0, 32), (1, 8)), jnp.float32),
    }


def one_replica(args):
    acts_r, weight_r, cot_r = args
    keys_r = jnp.dot(acts_r, weight_r, preferred_element_type=jnp.float32).astype(jnp.bfloat16)
    back_r = lax.dot_general(cot_r, weight_r, (((1,), (1,)), ((), ())), preferred_element_type=jnp.float32).astype(jnp.bfloat16)
    grad_r = lax.dot_general(acts_r, cot_r, (((0,), (0,)), ((), ())), preferred_element_type=jnp.float32)
    grad_r = (grad_r * (TOKENS_REP ** -0.5)).astype(jnp.bfloat16)
    return keys_r, grad_r, back_r


def reference(acts, key_weight, cotangent, frag_local, frag_anchor, frag_moment, frag_pending):
    keys, key_grad, act_grad = lax.map(one_replica, (acts, key_weight, cotangent))
    local_sum = jnp.sum(frag_local.astype(jnp.float32), axis=0)
    pending_next = frag_anchor - local_sum / REPS
    moment_next = 0.9 * frag_moment + frag_pending
    anchor_next = frag_anchor - 0.7 * (frag_pending + 0.9 * moment_next)
    shared = anchor_next.astype(jnp.bfloat16).astype(jnp.float32)
    local_next = (0.5 * frag_local.astype(jnp.float32) + 0.5 * shared[None]).astype(jnp.bfloat16)
    return keys, key_grad, act_grad, local_next, anchor_next, moment_next, pending_next
```

```python
import functools

import jax
import jax.numpy as jnp
from jax import lax
from jax.experimental import pallas as pl
from jax.experimental.pallas import tpu as pltpu
from jax.sharding import PartitionSpec as P

MESH = pl.DeviceIdType.MESH
BF = jnp.bfloat16
F32 = jnp.float32

TOK = 256
D = 7168
KW = 512
FW = 1024
SH = 224
CH = 896
COLS = 128
GROUP_TOKENS = 8192
A1 = 160
A2 = SH - A1
R1 = 160
R2 = SH - R1
A1H, A2H = 80, 32
R1H, R2H = 80, 32

COUNTS = (
    ("a1z", 8), ("a1x", 16), ("a2x", 4), ("a2z", 32), ("sib", 8), ("dp", 8),
    ("r1h", 8), ("r1f", 8), ("r1z", 8), ("r2z", 32), ("r2h", 2), ("r2f", 2),
    ("oy", 6), ("os", 1), ("oy2", 3), ("oy3", 3), ("op", 1),
)
BASE = {}
TOTAL = 0
for _name, _n in COUNTS:
    BASE[_name] = TOTAL
    TOTAL += _n
LOADS = 7
ORDER = None


def default_order():
    o = []
    o += ["own", "outer_send"]
    o += [("dw", 0), ("dw", 1), "a2L", "a2R", ("dw", 2), ("dw", 3), ("z1", 1), ("x1L", 0), ("x1R", 0)]
    o += [("pair", 0), ("pair", 1), ("r1a", 0), ("dw", 4), ("dw", 5), "outer_y"]
    o += [("pair", 2), ("pair", 3), ("r1a", 1), "a2F", ("dw", 6), ("dw", 7)]
    o += [("z1", 2), ("x1L", 1), ("x1R", 1)]
    o += [("z2", 1, 0), ("z2", 1, 1), ("z2", 1, 2), ("z2", 1, 3)]
    o += [("pair", 4), ("pair", 5), ("r1a", 2), ("pair", 6), ("pair", 7), ("r1a", 3)]
    o += [("r2z", 0, 0), ("r2z", 0, 1), ("r2z", 0, 2), ("r2z", 0, 3)]
    o += [("x1F", 0), ("sibown", 0)]
    o += [("r1b", 0), ("z1", 3), ("x1L", 2), ("x1R", 2), ("r2z", 1, 0), ("r2z", 1, 1), ("r2z", 1, 2), ("r2z", 1, 3)]
    o += [("comp", 0), ("z2", 2, 0), ("z2", 2, 1), ("z2", 2, 2), ("z2", 2, 3)]
    o += [("r1b", 1), ("r1c", 0), "outer_mid", ("x1F", 1), ("sib", 1)]
    o += [("r2z", 2, 0), ("r2z", 2, 1), ("r2z", 2, 2), ("r2z", 2, 3), ("x1L", 3), ("x1R", 3), ("comp", 1)]
    o += [("r1b", 2), ("r1c", 1), ("x1F", 2), ("sib", 2)]
    o += [("z2", 3, 0), ("z2", 3, 1), ("z2", 3, 2), ("z2", 3, 3)]
    o += [("r2z", 3, 0), ("r2z", 3, 1), ("r2z", 3, 2), ("r2z", 3, 3), "r2a", ("r1b", 3), ("comp", 2)]
    o += [("r1c", 2), "r2b", ("x1F", 3), ("sib", 3), "outer_end", ("r1c", 3), "r2c", ("comp", 3)]
    return o


def kernel(
    acts_h, kw_h, cot_h, fl_h, anchor_h, moment_h, pending_h,
    keys_o, grad_o, back_o, local_o, anchor_o, moment_o, pending_o,
    acts, cot, fl, anchor, moment, pending,
    w, d, rb, r1h, r1f, r1z, r2z, r2h, r2f,
    acc, back, keys_v, grad_v, local_v, anchor_v, moment_v, pending_v,
    ry, shared, part_out, part_in,
    send_sem, recv_sem, load_sem, out_sem,
):
    rep, me = lax.axis_index("rep"), lax.axis_index("fsdp")
    zh, y = rep // 4, rep % 4
    z, x, c = me // 8, (me // 2) % 4, me % 2
    xl, xr, xo = (x + 3) % 4, (x + 1) % 4, (x + 2) % 4
    at_z0, at_z1, at_z2, at_z3 = z == 0, z == 1, z == 2, z == 3
    low, high = z == 0, z == 3

    def table(a, b, e, f):
        return jnp.where(at_z0, a, jnp.where(at_z1, b, jnp.where(at_z2, e, f)))

    near = [z, table(1, 0, 3, 2), table(2, 2, 1, 1), table(3, 3, 0, 0)]
    far = near[::-1]

    def dev(tz, tx, tc):
        return (rep, tz * 8 + tx * 2 + tc)

    right, left = dev(z, xr, c), dev(z, xl, c)
    up, down = dev(jnp.minimum(z + 1, 3), x, c), dev(jnp.maximum(z - 1, 0), x, c)
    sibling = dev(z, x, 1 - c)
    other_zh = ((1 - zh) * 4 + y, me)

    def chip(tz, tx):
        return tz * 4 + tx

    pending_sends = []

    def remote(src, dst, name, index, to):
        return pltpu.make_async_remote_copy(
            src_ref=src, dst_ref=dst,
            send_sem=send_sem.at[BASE[name] + index], recv_sem=recv_sem.at[BASE[name] + index],
            device_id=to, device_id_type=MESH,
        )

    def send(src, dst, name, index, to, when=None):
        copy = remote(src, dst, name, index, to)
        if when is None:
            copy.start()
        else:
            pl.when(when)(copy.start)
        pending_sends.append((copy, when))

    def recv(dst, name, index, when=None):
        copy = remote(dst, dst, name, index, sibling)
        if when is None:
            copy.wait_recv()
        else:
            pl.when(when)(copy.wait_recv)

    loads = [
        (kw_h, w.at[chip(z, x), c]), (cot_h, cot), (acts_h, acts), (fl_h, fl),
        (anchor_h, anchor), (moment_h, moment), (pending_h, pending),
    ]
    loads = [pltpu.make_async_copy(s, t, load_sem.at[i]) for i, (s, t) in enumerate(loads)]
    for copy in loads:
        copy.start()

    barrier = pltpu.get_barrier_semaphore()

    def greet(to):
        pl.semaphore_signal(barrier, inc=1, device_id=to, device_id_type=MESH)

    for to in (left, right, sibling, other_zh):
        greet(to)
    for k in range(1, 4):
        greet((zh * 4 + (y + k) % 4, me))

    @pl.when(z < 3)
    def _():
        greet(up)

    @pl.when(z > 0)
    def _():
        greet(down)

    loads[0].wait()
    pl.semaphore_wait(barrier, 8 + jnp.where(low | high, 0, 1))

    not_low, not_high = z > 0, z < 3

    def wr(tz, tx, start, size):
        return w.at[chip(tz, tx), c, pl.ds(start, size)]

    def a1_round(tz):
        for i, to in ((0, right), (1, left)):
            send(wr(tz, x, 0, A1), wr(tz, x, 0, A1), "a1x", tz * 4 + i, to)

    def a2_along(tz, tx, ups, downs):
        for i, to, ok in ((0, up, ups), (1, down, downs)):
            send(wr(tz, tx, A1, A2), wr(tz, tx, A1, A2), "a2z", (i * 4 + tz) * 4 + tx, to, ok)

    def own():
        for i, to in ((0, right), (1, left)):
            send(wr(z, x, A1, A2), wr(z, x, A1, A2), "a2x", i, to)
        for i, to, ok in ((0, up, not_high), (1, down, not_low)):
            send(wr(z, x, 0, A1), wr(z, x, 0, A1), "a1z", i * 4 + z, to, ok)
        a1_round(z)
        a2_along(z, x, not_high, not_low)

    def z1(j):
        tz = near[j]
        rising = tz < z
        recv(wr(tz, x, 0, A1), "a1z", jnp.where(rising, 0, 4) + tz)
        piece = wr(tz, x, 0, A1)
        send(piece, piece, "a1z", tz, up, rising & not_high)
        send(piece, piece, "a1z", 4 + tz, down, (tz > z) & not_low)
        a1_round(tz)

    def x1L(j):
        tz = near[j]
        recv(wr(tz, xl, 0, A1), "a1x", tz * 4)
        piece = wr(tz, xl, 0, A1H)
        send(piece, piece, "a1x", tz * 4 + 2, right)

    def x1R(j):
        tz = near[j]
        recv(wr(tz, xr, 0, A1), "a1x", tz * 4 + 1)
        piece = wr(tz, xr, A1H, A1 - A1H)
        send(piece, piece, "a1x", tz * 4 + 3, left)

    def x1F(j):
        tz = near[j]
        recv(wr(tz, xo, 0, A1H), "a1x", tz * 4 + 2)
        recv(wr(tz, xo, A1H, A1 - A1H), "a1x", tz * 4 + 3)

    def a2L():
        recv(wr(z, xl, A1, A2), "a2x", 0)
        piece = wr(z, xl, A1, A2H)
        send(piece, piece, "a2x", 2, right)
        a2_along(z, xl, not_high, not_low)

    def a2R():
        recv(wr(z, xr, A1, A2), "a2x", 1)
        piece = wr(z, xr, A1 + A2H, A2 - A2H)
        send(piece, piece, "a2x", 3, left)
        a2_along(z, xr, not_high, not_low)

    def a2F():
        recv(wr(z, xo, A1, A2H), "a2x", 2)
        recv(wr(z, xo, A1 + A2H, A2 - A2H), "a2x", 3)
        a2_along(z, xo, not_high, not_low)

    def z2(j, p):
        tz, tx = near[j], (x, xl, xr, xo)[p]
        rising = tz < z
        recv(wr(tz, tx, A1, A2), "a2z", (jnp.where(rising, 0, 4) + tz) * 4 + tx)
        a2_along(tz, tx, rising & not_high, (tz > z) & not_low)

    def half_of(j, p):
        tz, px = near[j], x // 2 if p == 0 else 1 - x // 2
        return tz * 2 + px, chip(tz, px * 2)

    def sib(j):
        for p in range(2):
            index, first = half_of(j, p)
            piece = w.at[pl.ds(first, 2), c]
            send(piece, piece, "sib", index, sibling)

    def comp(j):
        for p in range(2):
            index, first = half_of(j, p)
            recv(w.at[pl.ds(first, 2), 1 - c], "sib", index)
            col = pl.multiple_of(index * CH, CH)
            rows = w[pl.ds(first, 2)].reshape(CH, KW)
            got = jnp.dot(acts[:, pl.ds(col, CH)], rows, preferred_element_type=F32)
            if j == 0 and p == 0:
                acc[...] = got
            else:
                acc[...] += got
            back[:, pl.ds(col, CH)] = lax.dot_general(
                cot[...], rows, (((1,), (1,)), ((), ())), preferred_element_type=F32
            ).astype(BF)
            out = pltpu.make_async_copy(
                back.at[:, pl.ds(col, CH)], back_o.at[:, pl.ds(col, CH)], out_sem.at[j * 2 + p]
            )
            out.start()
            outs.append(out)

    outs = []

    def grad_chunk(n):
        tz, px = far[n // 2], 1 - x // 2 if n % 2 == 0 else x // 2
        return tz * 2 + px, chip(tz, px * 2)

    def dw(n):
        if n == 0:
            loads[1].wait()
            loads[2].wait()
        index, first = grad_chunk(n)
        col = pl.multiple_of(index * CH, CH)
        got = lax.dot_general(
            acts[:, pl.ds(col, CH)], cot[...], (((0,), (0,)), ((), ())), preferred_element_type=F32
        )
        d[pl.ds(first, 2)] = got.astype(BF).reshape(2, 2, SH, KW)
        send(d.at[pl.ds(first, 2), 1 - c], rb.at[pl.ds(first, 2)], "dp", index, sibling)

    def pair(n):
        index, first = grad_chunk(n)
        recv(rb.at[pl.ds(first, 2)], "dp", index)
        for k in range(2):
            d[first + k, c] = (d[first + k, c].astype(F32) + rb[first + k].astype(F32)).astype(BF)

    def add(tz, tx, start, size, *others):
        here = (chip(tz, tx), c, pl.ds(start, size))
        total = d[here].astype(F32)
        for ref in others:
            total = total + ref[...].astype(F32)
        d[here] = total.astype(BF)

    def dr(tz, tx, start, size):
        return d.at[chip(tz, tx), c, pl.ds(start, size)]

    def r1a(i):
        tz = far[i]
        send(dr(tz, xo, 0, R1H), r1h.at[tz, 0, pl.ds(0, R1H)], "r1h", tz * 2, right)
        send(dr(tz, xo, R1H, R1 - R1H), r1h.at[tz, 1, pl.ds(0, R1 - R1H)], "r1h", tz * 2 + 1, left)

    def r1b(i):
        tz = far[i]
        from_left, from_right = r1h.at[tz, 0, pl.ds(0, R1H)], r1h.at[tz, 1, pl.ds(0, R1 - R1H)]
        recv(from_left, "r1h", tz * 2)
        add(tz, xr, 0, R1H, from_left)
        send(dr(tz, xr, 0, R1), r1f.at[tz, 0], "r1f", tz * 2, right)
        recv(from_right, "r1h", tz * 2 + 1)
        add(tz, xl, R1H, R1 - R1H, from_right)
        send(dr(tz, xl, 0, R1), r1f.at[tz, 1], "r1f", tz * 2 + 1, left)

    scale = GROUP_TOKENS ** -0.5

    def along(tz, tx, start, size, buffer, name, index, extra):
        rising = tz > z
        first = jnp.where(rising, low, high)
        got = buffer(jnp.where(rising, 0, 1))
        where = index(jnp.where(rising, 0, 1))

        @pl.when(first)
        def _():
            if extra:
                add(tz, tx, start, size, *extra)

        @pl.when(jnp.logical_not(first))
        def _():
            recv(got, name, where)
            add(tz, tx, start, size, got, *extra)

        piece = dr(tz, tx, start, size)
        send(piece, got, name, where, up, rising)
        send(piece, got, name, where, down, jnp.logical_not(rising))

    def end(tx, start, size, buffer, name, index, extra, store):
        for ok, places in ((low, (1,)), (high, (0,)), (not_low & not_high, (0, 1))):
            @pl.when(ok)
            def _():
                for i in places:
                    recv(buffer(i), name, index(i))
                total = d[chip(z, tx), c, pl.ds(start, size)].astype(F32)
                for ref in [buffer(i) for i in places] + extra:
                    total = total + ref[...].astype(F32)
                store(total)

    def r1c(i):
        tz = far[i]
        recv(r1f.at[tz, 0], "r1f", tz * 2)
        recv(r1f.at[tz, 1], "r1f", tz * 2 + 1)
        extra = [r1f.at[tz, 0], r1f.at[tz, 1]]

        def buffer(k):
            return r1z.at[k, tz]

        def index(k):
            return k * 4 + tz

        if i < 3:
            along(tz, x, 0, R1, buffer, "r1z", index, extra)
        else:
            def store(total):
                grad_v[pl.ds(0, R1)] = (total * scale).astype(BF)

            end(x, 0, R1, buffer, "r1z", index, extra, store)

    def r2z_step(i, p):
        tz, tx = far[i], (xo, xl, xr, x)[p]

        def buffer(k):
            return r2z.at[k, tz, tx]

        def index(k):
            return (k * 4 + tz) * 4 + tx

        if i < 3:
            along(tz, tx, R1, R2, buffer, "r2z", index, [])
        else:
            def store(total):
                d[chip(z, tx), c, pl.ds(R1, R2)] = total.astype(BF)

            end(tx, R1, R2, buffer, "r2z", index, [], store)

    def r2a():
        send(dr(z, xo, R1, R2H), r2h.at[0, pl.ds(0, R2H)], "r2h", 0, right)
        send(dr(z, xo, R1 + R2H, R2 - R2H), r2h.at[1, pl.ds(0, R2 - R2H)], "r2h", 1, left)

    def r2b():
        from_left, from_right = r2h.at[0, pl.ds(0, R2H)], r2h.at[1, pl.ds(0, R2 - R2H)]
        recv(from_left, "r2h", 0)
        add(z, xr, R1, R2H, from_left)
        send(dr(z, xr, R1, R2), r2f.at[0], "r2f", 0, right)
        recv(from_right, "r2h", 1)
        add(z, xl, R1 + R2H, R2 - R2H, from_right)
        send(dr(z, xl, R1, R2), r2f.at[1], "r2f", 1, left)

    def r2c():
        recv(r2f.at[0], "r2f", 0)
        recv(r2f.at[1], "r2f", 1)
        total = d[chip(z, x), c, pl.ds(R1, R2)].astype(F32) + r2f[0].astype(F32) + r2f[1].astype(F32)
        grad_v[pl.ds(R1, R2)] = (total * scale).astype(BF)

    def outer_send():
        for copy in loads[3:]:
            copy.wait()
        for k in range(1, 4):
            ty = (y + k) % 4
            for h in range(2):
                send(
                    fl.at[:, pl.ds(pl.multiple_of((h * 4 + ty) * COLS, COLS), COLS)],
                    ry.at[k - 1, h], "oy", (k - 1) * 2 + h, (zh * 4 + ty, me),
                )
        moment_next = 0.9 * moment[...] + pending[...]
        anchor_next = anchor[...] - 0.7 * (pending[...] + 0.9 * moment_next)
        moment_v[...] = moment_next
        anchor_v[...] = anchor_next
        shared[zh, y] = anchor_next.astype(BF)
        send(shared.at[zh, y], shared.at[zh, y], "os", 0, other_zh)
        for k in range(1, 4):
            ty = (y + k) % 4
            send(shared.at[zh, y], shared.at[zh, y], "oy2", k - 1, (zh * 4 + ty, me))

    def outer_y():
        for k in range(1, 4):
            for h in range(2):
                recv(ry.at[k - 1, h], "oy", (k - 1) * 2 + h)
        recv(shared.at[1 - zh, y], "os", 0)
        for k in range(1, 4):
            ty = (y + k) % 4
            send(shared.at[1 - zh, y], shared.at[1 - zh, y], "oy3", k - 1, (zh * 4 + ty, me))

        def local(h):
            total = fl[:, pl.ds(pl.multiple_of((h * 4 + y) * COLS, COLS), COLS)].astype(F32)
            for k in range(3):
                total = total + ry[k, h].astype(F32)
            return total

        part_out[...] = local(1 - zh).astype(BF)
        send(part_out, part_in, "op", 0, other_zh)
        pending_v[...] = local(zh)

    def outer_mid():
        recv(part_in, "op", 0)
        pending_v[...] = anchor[...] - (pending_v[...] + part_in[...].astype(F32)) / 8

    def outer_end():
        for k in range(1, 4):
            ty = (y + 4 - k) % 4
            recv(shared.at[zh, ty], "oy2", k - 1)
            recv(shared.at[1 - zh, ty], "oy3", k - 1)
        for h in range(2):
            for q in range(4):
                cols = pl.ds((h * 4 + q) * COLS, COLS)
                local_v[:, cols] = (0.5 * fl[:, cols].astype(F32) + 0.5 * shared[h, q].astype(F32)).astype(BF)

    actions = {
        "own": own, "z1": z1, "x1L": x1L, "x1R": x1R, "x1F": x1F, "a2L": a2L, "a2R": a2R, "a2F": a2F,
        "z2": z2, "sib": sib, "sibown": sib, "comp": comp, "dw": dw, "pair": pair, "r1a": r1a, "r1b": r1b, "r1c": r1c,
        "r2z": r2z_step, "r2a": r2a, "r2b": r2b, "r2c": r2c,
        "outer_send": outer_send, "outer_y": outer_y, "outer_mid": outer_mid, "outer_end": outer_end,
    }
    for item in ORDER or default_order():
        name, *args = item if isinstance(item, tuple) else (item,)
        actions[name](*args)

    keys_v[...] = acc[...].astype(BF)
    for i, (s, t) in enumerate((
        (keys_v, keys_o), (grad_v, grad_o), (local_v, local_o),
        (anchor_v, anchor_o), (moment_v, moment_o), (pending_v, pending_o),
    )):
        out = pltpu.make_async_copy(s, t, out_sem.at[8 + i])
        out.start()
        outs.append(out)
    for out in outs:
        out.wait()
    for copy, when in pending_sends:
        if when is None:
            copy.wait_send()
        else:
            pl.when(when)(copy.wait_send)


def on_device(acts, key_weight, cotangent, frag_local, anchor, moment, pending):
    any_space = pl.BlockSpec(memory_space=pl.ANY)
    vm = pltpu.VMEM
    outs = pl.pallas_call(
        kernel,
        out_shape=[
            jax.ShapeDtypeStruct((TOK, KW), BF), jax.ShapeDtypeStruct((SH, KW), BF),
            jax.ShapeDtypeStruct((TOK, D), BF), jax.ShapeDtypeStruct((SH, FW), BF),
            jax.ShapeDtypeStruct((SH, COLS), F32), jax.ShapeDtypeStruct((SH, COLS), F32),
            jax.ShapeDtypeStruct((SH, COLS), F32),
        ],
        in_specs=[any_space] * 7,
        out_specs=[any_space] * 7,
        scratch_shapes=[
            vm((TOK, D), BF), vm((TOK, KW), BF), vm((SH, FW), BF),
            vm((SH, COLS), F32), vm((SH, COLS), F32), vm((SH, COLS), F32),
            vm((16, 2, SH, KW), BF), vm((16, 2, SH, KW), BF), vm((16, SH, KW), BF),
            vm((4, 2, max(R1H, R1 - R1H), KW), BF), vm((4, 2, R1, KW), BF), vm((2, 4, R1, KW), BF),
            vm((2, 4, 4, R2, KW), BF), vm((2, max(R2H, R2 - R2H), KW), BF), vm((2, R2, KW), BF),
            vm((TOK, KW), F32), vm((TOK, D), BF), vm((TOK, KW), BF), vm((SH, KW), BF), vm((SH, FW), BF),
            vm((SH, COLS), F32), vm((SH, COLS), F32), vm((SH, COLS), F32),
            vm((3, 2, SH, COLS), BF), vm((2, 4, SH, COLS), BF), vm((SH, COLS), BF), vm((SH, COLS), BF),
            pltpu.SemaphoreType.DMA((TOTAL,)), pltpu.SemaphoreType.DMA((TOTAL,)),
            pltpu.SemaphoreType.DMA((LOADS,)), pltpu.SemaphoreType.DMA((14,)),
        ],
        name="window",
        compiler_params=pltpu.CompilerParams(
            collective_id=1, has_side_effects=True, vmem_limit_bytes=56 * 2**20
        ),
    )(acts[0], key_weight[0], cotangent[0], frag_local[0], anchor, moment, pending)
    keys, grad, back, local, anchor_next, moment_next, pending_next = outs
    return (keys[None], grad[None], back[None], local[None], anchor_next, moment_next, pending_next)


def solution(mesh):
    wide, flat = P("rep", "fsdp", None), P("fsdp", "rep")
    return jax.shard_map(
        on_device,
        mesh=mesh,
        in_specs=(wide,) * 4 + (flat,) * 3,
        out_specs=(wide,) * 4 + (flat,) * 3,
        check_vma=False,
    )
```

```python
import functools

import jax
import jax.numpy as jnp
from jax import lax
from jax.experimental import pallas as pl
from jax.experimental.pallas import tpu as pltpu
from jax.sharding import PartitionSpec as P

MESH = pl.DeviceIdType.MESH
BF = jnp.bfloat16
F32 = jnp.float32

TOK = 256
D = 7168
KW = 512
FW = 1024
SH = 224
CH = 896
COLS = 128
GROUP_TOKENS = 8192

COUNTS = (
    ("a1z", 8), ("a1x", 16), ("a2x", 4), ("a2z", 32), ("sib", 8), ("dp", 8),
    ("r1h", 8), ("r1f", 8), ("r1z", 8), ("r2z", 32), ("r2h", 2), ("r2f", 2),
    ("oy", 6), ("os", 1), ("oy2", 3), ("oy3", 3), ("op", 1),
)
BASE = {}
TOTAL = 0
for _name, _n in COUNTS:
    BASE[_name] = TOTAL
    TOTAL += _n
LOADS = 7


ENDS = (
    ("own",), ("dw", 0), ("dw", 2), ("pair", 0), ("dw", 3), ("outer_send",), ("r1a", 0), ("dw", 1), ("a2L",),
    ("pair", 2), ("a2R",), ("pair", 3), ("dw", 4), ("dw", 5), ("z1", 1), ("r1a", 1), ("pair", 1), ("r2z", 1, 0),
    ("r2z", 0, 0), ("r1bL", 0), ("x1L", 0), ("pair", 4), ("x1R", 0), ("r2z", 0, 3), ("r2z", 0, 2), ("a2F",),
    ("x1L", 1), ("z2", 1, 0), ("r2z", 1, 3), ("sib", 0, 0), ("r2z", 1, 1), ("r1a", 2), ("r2z", 1, 2), ("r2z", 0, 1),
    ("x1R", 1), ("outer_y",), ("z2", 1, 1), ("z2", 2, 0), ("r1bR", 0), ("dw", 6), ("z1", 2), ("pair", 6), ("z1", 3),
    ("outer_mid",), ("comp", 0, 0), ("x1F", 1), ("pair", 5), ("z2", 1, 3), ("r2z", 2, 1), ("dw", 7), ("x1L", 2),
    ("r2z", 2, 0), ("r1bR", 1), ("r1bL", 1), ("z2", 1, 2), ("r1c", 0), ("r1a", 3), ("r1bL", 2), ("x1F", 0),
    ("x1L", 3), ("r2z", 2, 2), ("z2", 2, 2), ("z2", 2, 1), ("sib", 1, 1), ("x1R", 2), ("sib", 2, 0), ("z2", 2, 3),
    ("outer_end",), ("pair", 7), ("r1c", 1), ("sib", 1, 0), ("r1bR", 2), ("sib", 0, 1), ("r2z", 3, 0), ("r2a",),
    ("r1bL", 3), ("comp", 1, 1), ("z2", 3, 0), ("comp", 1, 0), ("r2z", 2, 3), ("x1F", 2), ("z2", 3, 1),
    ("sib", 2, 1), ("x1R", 3), ("z2", 3, 3), ("comp", 2, 0), ("r2z", 3, 2), ("r1bR", 3), ("z2", 3, 2), ("r1c", 2),
    ("comp", 0, 1), ("comp", 2, 1), ("sib", 3, 0), ("r2bL",), ("r2z", 3, 1), ("x1F", 3), ("r2bR",), ("sib", 3, 1),
    ("comp", 3, 0), ("comp", 3, 1), ("r2z", 3, 3), ("r1c", 3), ("r2c",),
)
MIDDLE = (
    ("own",), ("dw", 4), ("outer_send",), ("dw", 0), ("dw", 2), ("a2R",), ("dw", 6), ("a2L",), ("z1", 1), ("z1", 2),
    ("dw", 5), ("pair", 2), ("pair", 0), ("pair", 5), ("z2", 2, 0), ("z2", 2, 1), ("r1a", 0), ("r1a", 1),
    ("z2", 1, 2), ("z2", 1, 0), ("x1R", 1), ("a2F",), ("outer_y",), ("z2", 1, 1), ("dw", 3), ("dw", 1), ("x1L", 1),
    ("pair", 4), ("z1", 3), ("r2z", 1, 0), ("x1L", 0), ("pair", 6), ("r2z", 0, 0), ("z2", 3, 0), ("dw", 7),
    ("pair", 1), ("r2z", 0, 2), ("sib", 1, 0), ("x1R", 2), ("outer_end",), ("x1R", 0), ("z2", 1, 3), ("sib", 0, 0),
    ("r1bR", 0), ("outer_mid",), ("x1F", 1), ("z2", 2, 3), ("x1L", 3), ("r2z", 0, 3), ("z2", 2, 2), ("z2", 3, 1),
    ("pair", 3), ("r1a", 2), ("comp", 0, 0), ("z2", 3, 2), ("x1L", 2), ("r2z", 2, 0), ("r2z", 1, 3), ("r1bL", 0),
    ("pair", 7), ("x1F", 0), ("r2z", 1, 2), ("r2z", 2, 2), ("r2z", 1, 1), ("sib", 1, 1), ("r1bL", 1), ("r2z", 0, 1),
    ("x1F", 2), ("r1a", 3), ("sib", 0, 1), ("r1bR", 1), ("sib", 2, 1), ("r1bR", 2), ("r2z", 3, 0), ("r2z", 2, 3),
    ("x1R", 3), ("z2", 3, 3), ("r2a",), ("sib", 3, 0), ("comp", 1, 0), ("r1bR", 3), ("comp", 0, 1), ("sib", 2, 0),
    ("r1c", 0), ("r1bL", 2), ("r2z", 2, 1), ("r1bL", 3), ("comp", 1, 1), ("comp", 2, 1), ("comp", 3, 0), ("r1c", 1),
    ("r1c", 2), ("r2z", 3, 1), ("r2z", 3, 2), ("x1F", 3), ("comp", 2, 0), ("r2bR",), ("r2bL",), ("sib", 3, 1),
    ("r1c", 3), ("r2z", 3, 3), ("comp", 3, 1), ("r2c",),
)
ORDER = (ENDS, MIDDLE)


def kernel(
    order, A1, R1, acts_h, kw_h, cot_h, fl_h, anchor_h, moment_h, pending_h,
    keys_o, grad_o, back_o, local_o, anchor_o, moment_o, pending_o,
    acts, cot, fl, anchor, moment, pending,
    w, d, rb, r1h, r1f, r1z, r2z, r2h, r2f,
    acc, ry, shared, part_out, part_in,
    send_sem, recv_sem, load_sem,
):
    A2, R2 = SH - A1, SH - R1
    A1H, A2H, R1H, R2H = (n // 32 * 16 for n in (A1, A2, R1, R2))
    rep, me = lax.axis_index("rep"), lax.axis_index("fsdp")
    zh, y = rep // 4, rep % 4
    z, x, c = me // 8, (me // 2) % 4, me % 2
    xl, xr, xo = (x + 3) % 4, (x + 1) % 4, (x + 2) % 4
    at_z0, at_z1, at_z2, at_z3 = z == 0, z == 1, z == 2, z == 3
    low, high = z == 0, z == 3

    def table(a, b, e, f):
        return jnp.where(at_z0, a, jnp.where(at_z1, b, jnp.where(at_z2, e, f)))

    near = [z, table(1, 0, 3, 2), table(2, 2, 1, 1), table(3, 3, 0, 0)]
    far = near[::-1]

    def dev(tz, tx, tc):
        return (rep, tz * 8 + tx * 2 + tc)

    right, left = dev(z, xr, c), dev(z, xl, c)
    up, down = dev(jnp.minimum(z + 1, 3), x, c), dev(jnp.maximum(z - 1, 0), x, c)
    sibling = dev(z, x, 1 - c)
    other_zh = ((1 - zh) * 4 + y, me)

    def chip(tz, tx):
        return tz * 4 + tx

    pending_sends = []

    def remote(src, dst, name, index, to):
        return pltpu.make_async_remote_copy(
            src_ref=src, dst_ref=dst,
            send_sem=send_sem.at[BASE[name] + index], recv_sem=recv_sem.at[BASE[name] + index],
            device_id=to, device_id_type=MESH,
        )

    def send(src, dst, name, index, to):
        copy = remote(src, dst, name, index, to)
        copy.start()
        pending_sends.append(copy)

    def recv(dst, name, index):
        remote(dst, dst, name, index, sibling).wait_recv()

    loads = [
        (kw_h, w.at[chip(z, x), c]), (cot_h, cot), (acts_h, acts), (fl_h, fl),
        (anchor_h, anchor), (moment_h, moment), (pending_h, pending),
    ]
    loads = [pltpu.make_async_copy(s, t, load_sem.at[i]) for i, (s, t) in enumerate(loads)]
    for copy in loads:
        copy.start()

    barrier = pltpu.get_barrier_semaphore()

    def greet(to):
        pl.semaphore_signal(barrier, inc=1, device_id=to, device_id_type=MESH)

    for to in (left, right, sibling, other_zh):
        greet(to)
    for k in range(1, 4):
        greet((zh * 4 + (y + k) % 4, me))

    @pl.when(z < 3)
    def _():
        greet(up)

    @pl.when(z > 0)
    def _():
        greet(down)

    loads[0].wait()
    pl.semaphore_wait(barrier, 8 + jnp.where(low | high, 0, 1))

    inner = dev(jnp.where(low, 1, 2), x, c)

    def body(is_middle, order):
        def wr(tz, tx, start, size):
            return w.at[chip(tz, tx), c, pl.ds(start, size)]

        def a1_round(tz):
            for i, to in ((0, right), (1, left)):
                send(wr(tz, x, 0, A1), wr(tz, x, 0, A1), "a1x", tz * 4 + i, to)

        pending_sends.clear()
        tokens_here = []
        starts = ((0, up), (1, down)) if is_middle else ((jnp.where(low, 0, 1), inner),)

        def onward(tz):
            rising = tz < z
            return jnp.where(rising, 0, 1), dev(jnp.where(rising, z + 1, z - 1), x, c)

        def a2_along(tz, tx, ways):
            for i, to in ways:
                send(wr(tz, tx, A1, A2), wr(tz, tx, A1, A2), "a2z", (i * 4 + tz) * 4 + tx, to)

        def own():
            for i, to in ((0, right), (1, left)):
                send(wr(z, x, A1, A2), wr(z, x, A1, A2), "a2x", i, to)
            for i, to in starts:
                send(wr(z, x, 0, A1), wr(z, x, 0, A1), "a1z", i * 4 + z, to)
            a1_round(z)
            a2_along(z, x, starts)

        def z1(j):
            tz = near[j]
            rising = tz < z
            recv(wr(tz, x, 0, A1), "a1z", jnp.where(rising, 0, 4) + tz)
            piece = wr(tz, x, 0, A1)
            if is_middle:
                way, to = onward(tz)
                send(piece, piece, "a1z", way * 4 + tz, to)
            a1_round(tz)

        def x1L(j):
            tz = near[j]
            recv(wr(tz, xl, 0, A1), "a1x", tz * 4)
            piece = wr(tz, xl, 0, A1H)
            send(piece, piece, "a1x", tz * 4 + 2, right)

        def x1R(j):
            tz = near[j]
            recv(wr(tz, xr, 0, A1), "a1x", tz * 4 + 1)
            piece = wr(tz, xr, A1H, A1 - A1H)
            send(piece, piece, "a1x", tz * 4 + 3, left)

        def x1F(j):
            tz = near[j]
            recv(wr(tz, xo, 0, A1H), "a1x", tz * 4 + 2)
            recv(wr(tz, xo, A1H, A1 - A1H), "a1x", tz * 4 + 3)

        def a2L():
            recv(wr(z, xl, A1, A2), "a2x", 0)
            piece = wr(z, xl, A1, A2H)
            send(piece, piece, "a2x", 2, right)
            a2_along(z, xl, starts)

        def a2R():
            recv(wr(z, xr, A1, A2), "a2x", 1)
            piece = wr(z, xr, A1 + A2H, A2 - A2H)
            send(piece, piece, "a2x", 3, left)
            a2_along(z, xr, starts)

        def a2F():
            recv(wr(z, xo, A1, A2H), "a2x", 2)
            recv(wr(z, xo, A1 + A2H, A2 - A2H), "a2x", 3)
            a2_along(z, xo, starts)

        def z2(j, p):
            tz, tx = near[j], (x, xl, xr, xo)[p]
            rising = tz < z
            recv(wr(tz, tx, A1, A2), "a2z", (jnp.where(rising, 0, 4) + tz) * 4 + tx)
            if is_middle:
                a2_along(tz, tx, (onward(tz),))

        def half_of(j, p):
            tz, px = near[j], x // 2 if p == 0 else 1 - x // 2
            return tz * 2 + px, chip(tz, px * 2)

        def sib(j, p):
            index, first = half_of(j, p)
            piece = w.at[pl.ds(first, 2), c]
            send(piece, piece, "sib", index, sibling)

        def await_tokens():
            if not tokens_here:
                loads[1].wait()
                loads[2].wait()
                tokens_here.append(True)

        def comp(j, p):
            await_tokens()
            index, first = half_of(j, p)
            recv(w.at[pl.ds(first, 2), 1 - c], "sib", index)
            col = pl.multiple_of(index * CH, CH)
            rows = w[pl.ds(first, 2)].reshape(CH, KW)
            got = jnp.dot(acts[:, pl.ds(col, CH)], rows, preferred_element_type=F32)
            if j == 0 and p == 0:
                acc[...] = got
            else:
                acc[...] += got
            back_o[:, pl.ds(col, CH)] = lax.dot_general(
                cot[...], rows, (((1,), (1,)), ((), ())), preferred_element_type=F32
            ).astype(BF)

        def grad_chunk(n):
            tz, px = far[n // 2], 1 - x // 2 if n % 2 == 0 else x // 2
            return tz * 2 + px, chip(tz, px * 2)

        def dw(n):
            await_tokens()
            index, first = grad_chunk(n)
            col = pl.multiple_of(index * CH, CH)
            got = lax.dot_general(
                acts[:, pl.ds(col, CH)], cot[...], (((0,), (0,)), ((), ())), preferred_element_type=F32
            )
            d[pl.ds(first, 2)] = got.astype(BF).reshape(2, 2, SH, KW)
            send(d.at[pl.ds(first, 2), 1 - c], rb.at[pl.ds(first, 2)], "dp", index, sibling)

        def pair(n):
            index, first = grad_chunk(n)
            recv(rb.at[pl.ds(first, 2)], "dp", index)
            for k in range(2):
                d[first + k, c] = (d[first + k, c].astype(F32) + rb[first + k].astype(F32)).astype(BF)

        def add(tz, tx, start, size, *others):
            here = (chip(tz, tx), c, pl.ds(start, size))
            total = d[here].astype(F32)
            for ref in others:
                total = total + ref[...].astype(F32)
            d[here] = total.astype(BF)

        def dr(tz, tx, start, size):
            return d.at[chip(tz, tx), c, pl.ds(start, size)]

        def r1a(i):
            tz = far[i]
            send(dr(tz, xo, 0, R1H), r1h.at[tz, 0, pl.ds(0, R1H)], "r1h", tz * 2, right)
            send(dr(tz, xo, R1H, R1 - R1H), r1h.at[tz, 1, pl.ds(0, R1 - R1H)], "r1h", tz * 2 + 1, left)

        def r1bL(i):
            tz = far[i]
            got = r1h.at[tz, 0, pl.ds(0, R1H)]
            recv(got, "r1h", tz * 2)
            add(tz, xr, 0, R1H, got)
            send(dr(tz, xr, 0, R1), r1f.at[tz, 0], "r1f", tz * 2, right)

        def r1bR(i):
            tz = far[i]
            got = r1h.at[tz, 1, pl.ds(0, R1 - R1H)]
            recv(got, "r1h", tz * 2 + 1)
            add(tz, xl, R1H, R1 - R1H, got)
            send(dr(tz, xl, 0, R1), r1f.at[tz, 1], "r1f", tz * 2 + 1, left)

        scale = GROUP_TOKENS ** -0.5

        def along(tz, tx, start, size, buffer, name, index, extra):
            rising = tz > z
            way = jnp.where(rising, 0, 1)
            got, where = buffer(way), index(way)
            if is_middle:
                recv(got, name, where)
                add(tz, tx, start, size, got, *extra)
            elif extra:
                add(tz, tx, start, size, *extra)
            to = dev(jnp.where(rising, z + 1, z - 1), x, c)
            send(dr(tz, tx, start, size), got, name, where, to)

        def end(tx, start, size, buffer, name, index, extra):
            ways = (0, 1) if is_middle else (jnp.where(low, 1, 0),)
            for i in ways:
                recv(buffer(i), name, index(i))
            total = d[chip(z, tx), c, pl.ds(start, size)].astype(F32)
            for ref in [buffer(i) for i in ways] + extra:
                total = total + ref[...].astype(F32)
            return total

        def r1c(i):
            tz = far[i]
            recv(r1f.at[tz, 0], "r1f", tz * 2)
            recv(r1f.at[tz, 1], "r1f", tz * 2 + 1)
            extra = [r1f.at[tz, 0], r1f.at[tz, 1]]

            def buffer(k):
                return r1z.at[k, tz]

            def index(k):
                return k * 4 + tz

            if i < 3:
                along(tz, x, 0, R1, buffer, "r1z", index, extra)
            else:
                total = end(x, 0, R1, buffer, "r1z", index, extra)
                grad_o[pl.ds(0, R1)] = (total * scale).astype(BF)

        def r2z_step(i, p):
            tz, tx = far[i], (xo, xl, xr, x)[p]

            def buffer(k):
                return r2z.at[k, tz, tx]

            def index(k):
                return (k * 4 + tz) * 4 + tx

            if i < 3:
                along(tz, tx, R1, R2, buffer, "r2z", index, [])
            else:
                total = end(tx, R1, R2, buffer, "r2z", index, [])
                d[chip(z, tx), c, pl.ds(R1, R2)] = total.astype(BF)

        def r2a():
            send(dr(z, xo, R1, R2H), r2h.at[0, pl.ds(0, R2H)], "r2h", 0, right)
            send(dr(z, xo, R1 + R2H, R2 - R2H), r2h.at[1, pl.ds(0, R2 - R2H)], "r2h", 1, left)

        def r2bL():
            got = r2h.at[0, pl.ds(0, R2H)]
            recv(got, "r2h", 0)
            add(z, xr, R1, R2H, got)
            send(dr(z, xr, R1, R2), r2f.at[0], "r2f", 0, right)

        def r2bR():
            got = r2h.at[1, pl.ds(0, R2 - R2H)]
            recv(got, "r2h", 1)
            add(z, xl, R1 + R2H, R2 - R2H, got)
            send(dr(z, xl, R1, R2), r2f.at[1], "r2f", 1, left)

        def r2c():
            recv(r2f.at[0], "r2f", 0)
            recv(r2f.at[1], "r2f", 1)
            total = d[chip(z, x), c, pl.ds(R1, R2)].astype(F32) + r2f[0].astype(F32) + r2f[1].astype(F32)
            grad_o[pl.ds(R1, R2)] = (total * scale).astype(BF)

        def outer_send():
            for copy in loads[3:]:
                copy.wait()
            for k in range(1, 4):
                ty = (y + k) % 4
                for h in range(2):
                    send(
                        fl.at[:, pl.ds(pl.multiple_of((h * 4 + ty) * COLS, COLS), COLS)],
                        ry.at[k - 1, h], "oy", (k - 1) * 2 + h, (zh * 4 + ty, me),
                    )
            moment_next = 0.9 * moment[...] + pending[...]
            anchor_next = anchor[...] - 0.7 * (pending[...] + 0.9 * moment_next)
            moment_o[...] = moment_next
            anchor_o[...] = anchor_next
            shared[zh, y] = anchor_next.astype(BF)
            send(shared.at[zh, y], shared.at[zh, y], "os", 0, other_zh)
            for k in range(1, 4):
                ty = (y + k) % 4
                send(shared.at[zh, y], shared.at[zh, y], "oy2", k - 1, (zh * 4 + ty, me))

        def outer_y():
            for k in range(1, 4):
                for h in range(2):
                    recv(ry.at[k - 1, h], "oy", (k - 1) * 2 + h)
            recv(shared.at[1 - zh, y], "os", 0)
            for k in range(1, 4):
                ty = (y + k) % 4
                send(shared.at[1 - zh, y], shared.at[1 - zh, y], "oy3", k - 1, (zh * 4 + ty, me))

            def local(h):
                total = fl[:, pl.ds(pl.multiple_of((h * 4 + y) * COLS, COLS), COLS)].astype(F32)
                for k in range(3):
                    total = total + ry[k, h].astype(F32)
                return total

            part_out[...] = local(1 - zh).astype(BF)
            send(part_out, part_in, "op", 0, other_zh)
            pending_o[...] = local(zh)

        def outer_mid():
            recv(part_in, "op", 0)
            pending_o[...] = anchor[...] - (pending_o[...] + part_in[...].astype(F32)) / 8

        def outer_end():
            for k in range(1, 4):
                ty = (y + 4 - k) % 4
                recv(shared.at[zh, ty], "oy2", k - 1)
                recv(shared.at[1 - zh, ty], "oy3", k - 1)
            for h in range(2):
                for q in range(4):
                    cols = pl.ds((h * 4 + q) * COLS, COLS)
                    local_o[:, cols] = (0.5 * fl[:, cols].astype(F32) + 0.5 * shared[h, q].astype(F32)).astype(BF)

        actions = {
            "own": own, "z1": z1, "x1L": x1L, "x1R": x1R, "x1F": x1F, "a2L": a2L, "a2R": a2R, "a2F": a2F,
            "z2": z2, "sib": sib, "comp": comp, "dw": dw, "pair": pair, "r1a": r1a, "r1bL": r1bL, "r1bR": r1bR, "r1c": r1c,
            "r2z": r2z_step, "r2a": r2a, "r2bL": r2bL, "r2bR": r2bR, "r2c": r2c,
            "outer_send": outer_send, "outer_y": outer_y, "outer_mid": outer_mid, "outer_end": outer_end,
        }
        for name, *args in order:
            actions[name](*args)
        keys_o[...] = acc[...].astype(BF)
        for copy in pending_sends:
            copy.wait_send()

    pl.when(low | high)(functools.partial(body, False, order[0]))
    pl.when(jnp.logical_not(low | high))(functools.partial(body, True, order[1]))


def finish(*refs):
    sems = refs[-1]
    copies = [pltpu.make_async_copy(s, t, sems.at[i]) for i, (s, t) in enumerate(zip(refs[:7], refs[7:14], strict=True))]
    for copy in copies:
        copy.start()
    for copy in copies:
        copy.wait()


def launch(acts, key_weight, cotangent, frag_local, anchor, moment, pending, order=ORDER, A1=144, R1=144, name='window', cid=1):
    R2 = SH - R1
    R1H, R2H = R1 // 32 * 16, R2 // 32 * 16
    any_space = pl.BlockSpec(memory_space=pl.ANY)
    arrays = (acts[0], key_weight[0], cotangent[0], frag_local[0], anchor, moment, pending)
    vm = pltpu.VMEM
    outs = pl.pallas_call(
        functools.partial(kernel, order, A1, R1),
        out_shape=[
            vm((TOK, KW), BF), vm((SH, KW), BF), vm((TOK, D), BF), vm((SH, FW), BF),
            vm((SH, COLS), F32), vm((SH, COLS), F32), vm((SH, COLS), F32),
        ],
        in_specs=[any_space] * 7,
        out_specs=[pl.BlockSpec(memory_space=vm)] * 7,
        scratch_shapes=[
            vm((TOK, D), BF), vm((TOK, KW), BF), vm((SH, FW), BF),
            vm((SH, COLS), F32), vm((SH, COLS), F32), vm((SH, COLS), F32),
            vm((16, 2, SH, KW), BF), vm((16, 2, SH, KW), BF), vm((16, SH, KW), BF),
            vm((4, 2, max(R1H, R1 - R1H), KW), BF), vm((4, 2, R1, KW), BF), vm((2, 4, R1, KW), BF),
            vm((2, 4, 4, R2, KW), BF), vm((2, max(R2H, R2 - R2H), KW), BF), vm((2, R2, KW), BF),
            vm((TOK, KW), F32), vm((3, 2, SH, COLS), BF), vm((2, 4, SH, COLS), BF), vm((SH, COLS), BF), vm((SH, COLS), BF),
            pltpu.SemaphoreType.DMA((TOTAL,)), pltpu.SemaphoreType.DMA((TOTAL,)),
            pltpu.SemaphoreType.DMA((LOADS,)),
        ],
        name=name,
        compiler_params=pltpu.CompilerParams(
            collective_id=cid, has_side_effects=True, vmem_limit_bytes=46 * 2**20
        ),
    )(*[pltpu.with_memory_space_constraint(a, pltpu.HBM) for a in arrays])
    outs = pl.pallas_call(
        finish,
        out_shape=[jax.ShapeDtypeStruct(o.shape, o.dtype) for o in outs],
        in_specs=[any_space] * 7,
        out_specs=[any_space] * 7,
        scratch_shapes=[pltpu.SemaphoreType.DMA((7,))],
        name="finish",
        compiler_params=pltpu.CompilerParams(vmem_limit_bytes=2**20),
    )(*[pltpu.with_memory_space_constraint(o, vm) for o in outs])
    keys, grad, back, local, anchor_next, moment_next, pending_next = outs
    return (keys[None], grad[None], back[None], local[None], anchor_next, moment_next, pending_next)


def on_device(*arrays):
    return launch(*arrays)


def solution(mesh):
    wide, flat = P("rep", "fsdp", None), P("fsdp", "rep")
    return jax.shard_map(
        on_device,
        mesh=mesh,
        in_specs=(wide,) * 4 + (flat,) * 3,
        out_specs=(wide,) * 4 + (flat,) * 3,
        check_vma=False,
    )
```

```python
import functools

import jax
import jax.numpy as jnp
from jax import lax
from jax.experimental import pallas as pl
from jax.experimental.pallas import tpu as pltpu
from jax.sharding import PartitionSpec as P

MESH = pl.DeviceIdType.MESH
BF = jnp.bfloat16
F32 = jnp.float32

TOK = 256
D = 7168
KW = 512
FW = 1024
SH = 224
CH = 896
COLS = 128
GROUP_TOKENS = 8192

COUNTS = (
    ("a1z", 8), ("a1x", 16), ("a2x", 4), ("a2z", 16), ("sib", 8), ("dp", 8),
    ("r1h", 8), ("r1f", 8), ("r1z", 8), ("r2z", 16), ("r2h", 2), ("r2f", 2),
    ("oy", 6), ("os", 1), ("oy2", 3), ("oy3", 3), ("op", 1),
)
BASE = {}
TOTAL = 0
for _name, _n in COUNTS:
    BASE[_name] = TOTAL
    TOTAL += _n
LOADS = 7


ENDS = (
    ("o2x",), ("o1z",), ("dw", 1), ("dw", 6), ("x1o", 0), ("dw", 2), ("dw", 0), ("dw", 5), ("a2L",), ("a2R",),
    ("pair", 2), ("pair", 0), ("pair", 1), ("r1a", 0), ("r2z", 0, 0), ("dw", 4), ("r1a", 1), ("x1R", 0), ("x1L", 0),
    ("z1", 1), ("pair", 4), ("r1bL", 0), ("x1o", 1), ("r2z", 0, 1), ("a2F",), ("outer_send",), ("dw", 3),
    ("r1bR", 0), ("z1", 2), ("g2", 1), ("pair", 3), ("r2z", 1, 0), ("dw", 7), ("sib", 0, 0), ("z1", 3), ("pair", 6),
    ("g2", 0), ("r1a", 2), ("pair", 5), ("x1o", 2), ("comp", 0, 0), ("outer_y",), ("r1bR", 1), ("x1L", 1),
    ("r2z", 2, 0), ("x1R", 1), ("x1o", 3), ("r2z", 1, 1), ("r1bL", 1), ("outer_end",), ("x1L", 2), ("x1R", 2),
    ("z2", 1, 1), ("pair", 7), ("z2", 1, 0), ("r1a", 3), ("x1F", 0), ("sib", 1, 0), ("x1F", 1), ("r1c", 0),
    ("x1R", 3), ("r1bR", 2), ("x1L", 3), ("sib", 0, 1), ("comp", 1, 0), ("r2z", 3, 0), ("r2z", 2, 1), ("r2a",),
    ("r1c", 1), ("z2", 2, 0), ("r1bL", 2), ("x1F", 2), ("r2z", 3, 1), ("z2", 2, 1), ("outer_mid",), ("sib", 2, 0),
    ("sib", 2, 1), ("sib", 1, 1), ("x1F", 3), ("comp", 0, 1), ("r1bR", 3), ("z2", 3, 0), ("r1bL", 3), ("z2", 3, 1),
    ("r1c", 2), ("sib", 3, 0), ("sib", 3, 1), ("comp", 1, 1), ("comp", 2, 1), ("r2bL",), ("r2bR",), ("comp", 3, 1),
    ("comp", 2, 0), ("comp", 3, 0), ("r1c", 3), ("r2c",),
)
MIDDLE = (
    ("o2x",), ("dw", 1), ("o1z",), ("dw", 0), ("outer_send",), ("x1o", 0), ("dw", 6), ("pair", 0), ("a2R",),
    ("z1", 1), ("r1a", 0), ("x1o", 1), ("z1", 2), ("pair", 1), ("a2L",), ("x1L", 0), ("g2", 1), ("dw", 4),
    ("z1", 3), ("r1bR", 0), ("x1R", 0), ("r2z", 0, 0), ("x1o", 3), ("dw", 7), ("r2z", 0, 1), ("z2", 2, 1),
    ("dw", 5), ("a2F",), ("pair", 4), ("dw", 2), ("pair", 6), ("x1o", 2), ("sib", 0, 0), ("g2", 0), ("z2", 1, 1),
    ("outer_y",), ("r1a", 2), ("pair", 7), ("pair", 2), ("dw", 3), ("pair", 5), ("x1L", 1), ("r1a", 1),
    ("r2z", 2, 0), ("x1F", 0), ("z2", 2, 0), ("comp", 0, 0), ("z2", 1, 0), ("x1R", 1), ("pair", 3), ("r1bL", 0),
    ("r1bR", 2), ("r1bL", 1), ("x1R", 3), ("x1R", 2), ("r2z", 1, 0), ("r1a", 3), ("x1L", 2), ("x1L", 3),
    ("sib", 0, 1), ("r2z", 2, 1), ("comp", 0, 1), ("z2", 3, 0), ("r1bL", 2), ("r2z", 1, 1), ("r2z", 3, 0),
    ("sib", 1, 0), ("r1bR", 1), ("z2", 3, 1), ("outer_end",), ("r2a",), ("sib", 3, 0), ("r1c", 0), ("x1F", 1),
    ("x1F", 2), ("r1bL", 3), ("sib", 1, 1), ("comp", 1, 0), ("comp", 3, 0), ("x1F", 3), ("sib", 2, 0),
    ("r2z", 3, 1), ("sib", 3, 1), ("r1bR", 3), ("comp", 1, 1), ("outer_mid",), ("r2bL",), ("r1c", 1), ("r1c", 2),
    ("sib", 2, 1), ("comp", 2, 0), ("r2bR",), ("comp", 3, 1), ("comp", 2, 1), ("r1c", 3), ("r2c",),
)
ORDER = (ENDS, MIDDLE)


def kernel(
    order, A1, R1, acts_h, kw_h, cot_h, fl_h, anchor_h, moment_h, pending_h,
    keys_o, grad_o, back_o, local_o, anchor_o, moment_o, pending_o,
    acts, cot, fl, anchor, moment, pending,
    w, d, rb, r1h, r1f, r1z, r2z, r2h, r2f,
    acc, ry, shared, part_out, part_in,
    send_sem, recv_sem, load_sem,
):
    A2, R2 = SH - A1, SH - R1
    A1H, A2H, R1H, R2H = (n // 32 * 16 for n in (A1, A2, R1, R2))
    rep, me = lax.axis_index("rep"), lax.axis_index("fsdp")
    zh, y = rep // 4, rep % 4
    z, x, c = me // 8, (me // 2) % 4, me % 2
    xl, xr, xo = (x + 3) % 4, (x + 1) % 4, (x + 2) % 4
    at_z0, at_z1, at_z2, at_z3 = z == 0, z == 1, z == 2, z == 3
    low, high = z == 0, z == 3

    def table(a, b, e, f):
        return jnp.where(at_z0, a, jnp.where(at_z1, b, jnp.where(at_z2, e, f)))

    near = [z, table(1, 0, 3, 2), table(2, 2, 1, 1), table(3, 3, 0, 0)]
    far = near[::-1]

    def dev(tz, tx, tc):
        return (rep, tz * 8 + tx * 2 + tc)

    right, left = dev(z, xr, c), dev(z, xl, c)
    up, down = dev(jnp.minimum(z + 1, 3), x, c), dev(jnp.maximum(z - 1, 0), x, c)
    sibling = dev(z, x, 1 - c)
    other_zh = ((1 - zh) * 4 + y, me)

    def chip(tz, tx):
        return tz, tx // 2, tx % 2

    pending_sends = []

    def remote(src, dst, name, index, to):
        return pltpu.make_async_remote_copy(
            src_ref=src, dst_ref=dst,
            send_sem=send_sem.at[BASE[name] + index], recv_sem=recv_sem.at[BASE[name] + index],
            device_id=to, device_id_type=MESH,
        )

    def send(src, dst, name, index, to):
        copy = remote(src, dst, name, index, to)
        copy.start()
        pending_sends.append(copy)

    def recv(dst, name, index):
        remote(dst, dst, name, index, sibling).wait_recv()

    loads = [
        (kw_h, w.at[(*chip(z, x), c)]), (cot_h, cot), (acts_h, acts), (fl_h, fl),
        (anchor_h, anchor), (moment_h, moment), (pending_h, pending),
    ]
    loads = [pltpu.make_async_copy(s, t, load_sem.at[i]) for i, (s, t) in enumerate(loads)]
    for copy in loads:
        copy.start()

    barrier = pltpu.get_barrier_semaphore()

    def greet(to):
        pl.semaphore_signal(barrier, inc=1, device_id=to, device_id_type=MESH)

    for to in (left, right, sibling, other_zh):
        greet(to)
    for k in range(1, 4):
        greet((zh * 4 + (y + k) % 4, me))

    @pl.when(z < 3)
    def _():
        greet(up)

    @pl.when(z > 0)
    def _():
        greet(down)

    loads[0].wait()
    pl.semaphore_wait(barrier, 8 + jnp.where(low | high, 0, 1))

    inner = dev(jnp.where(low, 1, 2), x, c)

    def body(is_middle, order):
        def wr(tz, tx, start, size):
            return w.at[(*chip(tz, tx), c, pl.ds(start, size))]

        def a1_round(tz):
            for i, to in ((0, right), (1, left)):
                send(wr(tz, x, 0, A1), wr(tz, x, 0, A1), "a1x", tz * 4 + i, to)

        pending_sends.clear()
        tokens_here = []
        starts = ((0, up), (1, down)) if is_middle else ((jnp.where(low, 0, 1), inner),)

        def onward(tz):
            rising = tz < z
            return jnp.where(rising, 0, 1), dev(jnp.where(rising, z + 1, z - 1), x, c)

        def two(tz, g):
            return w.at[tz, :, (x + g) % 2, c, pl.ds(A1, A2)]

        def a2_along(tz, g, ways):
            for i, to in ways:
                send(two(tz, g), two(tz, g), "a2z", (i * 4 + tz) * 2 + g, to)

        def o2x():
            for i, to in ((0, right), (1, left)):
                send(wr(z, x, A1, A2), wr(z, x, A1, A2), "a2x", i, to)

        def o1z():
            for i, to in starts:
                send(wr(z, x, 0, A1), wr(z, x, 0, A1), "a1z", i * 4 + z, to)

        def g2(g):
            a2_along(z, g, starts)

        def x1o(j):
            a1_round(near[j])

        def z1(j):
            tz = near[j]
            rising = tz < z
            recv(wr(tz, x, 0, A1), "a1z", jnp.where(rising, 0, 4) + tz)
            if is_middle:
                piece = wr(tz, x, 0, A1)
                way, to = onward(tz)
                send(piece, piece, "a1z", way * 4 + tz, to)

        def x1L(j):
            tz = near[j]
            recv(wr(tz, xl, 0, A1), "a1x", tz * 4)
            piece = wr(tz, xl, 0, A1H)
            send(piece, piece, "a1x", tz * 4 + 2, right)

        def x1R(j):
            tz = near[j]
            recv(wr(tz, xr, 0, A1), "a1x", tz * 4 + 1)
            piece = wr(tz, xr, A1H, A1 - A1H)
            send(piece, piece, "a1x", tz * 4 + 3, left)

        def x1F(j):
            tz = near[j]
            recv(wr(tz, xo, 0, A1H), "a1x", tz * 4 + 2)
            recv(wr(tz, xo, A1H, A1 - A1H), "a1x", tz * 4 + 3)

        def a2L():
            recv(wr(z, xl, A1, A2), "a2x", 0)
            piece = wr(z, xl, A1, A2H)
            send(piece, piece, "a2x", 2, right)

        def a2R():
            recv(wr(z, xr, A1, A2), "a2x", 1)
            piece = wr(z, xr, A1 + A2H, A2 - A2H)
            send(piece, piece, "a2x", 3, left)

        def a2F():
            recv(wr(z, xo, A1, A2H), "a2x", 2)
            recv(wr(z, xo, A1 + A2H, A2 - A2H), "a2x", 3)

        def z2(j, g):
            tz = near[j]
            recv(two(tz, g), "a2z", (jnp.where(tz < z, 0, 4) + tz) * 2 + g)
            if is_middle:
                a2_along(tz, g, (onward(tz),))

        def half_of(j, p):
            tz, px = near[j], x // 2 if p == 0 else 1 - x // 2
            return tz * 2 + px, (tz, px)

        def sib(j, p):
            index, first = half_of(j, p)
            piece = w.at[(*first, slice(None), c)]
            send(piece, piece, "sib", index, sibling)

        def await_tokens():
            if not tokens_here:
                loads[1].wait()
                loads[2].wait()
                tokens_here.append(True)

        def comp(j, p):
            await_tokens()
            index, first = half_of(j, p)
            recv(w.at[(*first, slice(None), 1 - c)], "sib", index)
            col = pl.multiple_of(index * CH, CH)
            rows = w[first].reshape(CH, KW)
            got = jnp.dot(acts[:, pl.ds(col, CH)], rows, preferred_element_type=F32)
            if j == 0 and p == 0:
                acc[...] = got
            else:
                acc[...] += got
            back_o[:, pl.ds(col, CH)] = lax.dot_general(
                cot[...], rows, (((1,), (1,)), ((), ())), preferred_element_type=F32
            ).astype(BF)

        def grad_chunk(n):
            tz, px = far[n // 2], 1 - x // 2 if n % 2 == 0 else x // 2
            return tz * 2 + px, (tz, px)

        def dw(n):
            await_tokens()
            index, first = grad_chunk(n)
            col = pl.multiple_of(index * CH, CH)
            got = lax.dot_general(
                acts[:, pl.ds(col, CH)], cot[...], (((0,), (0,)), ((), ())), preferred_element_type=F32
            )
            d[first] = got.astype(BF).reshape(2, 2, SH, KW)
            send(d.at[(*first, slice(None), 1 - c)], rb.at[first], "dp", index, sibling)

        def pair(n):
            index, first = grad_chunk(n)
            recv(rb.at[first], "dp", index)
            for k in range(2):
                d[(*first, k, c)] = (d[(*first, k, c)].astype(F32) + rb[(*first, k)].astype(F32)).astype(BF)

        def add(tz, tx, start, size, *others):
            here = (*chip(tz, tx), c, pl.ds(start, size))
            total = d[here].astype(F32)
            for ref in others:
                total = total + ref[...].astype(F32)
            d[here] = total.astype(BF)

        def dr(tz, tx, start, size):
            return d.at[(*chip(tz, tx), c, pl.ds(start, size))]

        def r1a(i):
            tz = far[i]
            send(dr(tz, xo, 0, R1H), r1h.at[tz, 0, pl.ds(0, R1H)], "r1h", tz * 2, right)
            send(dr(tz, xo, R1H, R1 - R1H), r1h.at[tz, 1, pl.ds(0, R1 - R1H)], "r1h", tz * 2 + 1, left)

        def r1bL(i):
            tz = far[i]
            got = r1h.at[tz, 0, pl.ds(0, R1H)]
            recv(got, "r1h", tz * 2)
            add(tz, xr, 0, R1H, got)
            send(dr(tz, xr, 0, R1), r1f.at[tz, 0], "r1f", tz * 2, right)

        def r1bR(i):
            tz = far[i]
            got = r1h.at[tz, 1, pl.ds(0, R1 - R1H)]
            recv(got, "r1h", tz * 2 + 1)
            add(tz, xl, R1H, R1 - R1H, got)
            send(dr(tz, xl, 0, R1), r1f.at[tz, 1], "r1f", tz * 2 + 1, left)

        scale = GROUP_TOKENS ** -0.5

        def gather_up(here, others):
            total = d[here].astype(F32)
            for ref in others:
                total = total + ref[...].astype(F32)
            return total

        def along(tz, here, buffer, name, index, extra):
            rising = tz > z
            way = jnp.where(rising, 0, 1)
            got, where = buffer(way), index(way)
            if is_middle:
                recv(got, name, where)
                d[here] = gather_up(here, [got, *extra]).astype(BF)
            elif extra:
                d[here] = gather_up(here, extra).astype(BF)
            to = dev(jnp.where(rising, z + 1, z - 1), x, c)
            send(d.at[here], got, name, where, to)

        def end(here, buffer, name, index, extra):
            ways = (0, 1) if is_middle else (jnp.where(low, 1, 0),)
            for i in ways:
                recv(buffer(i), name, index(i))
            return gather_up(here, [buffer(i) for i in ways] + extra)

        def r1c(i):
            tz = far[i]
            recv(r1f.at[tz, 0], "r1f", tz * 2)
            recv(r1f.at[tz, 1], "r1f", tz * 2 + 1)
            extra = [r1f.at[tz, 0], r1f.at[tz, 1]]
            here = (*chip(tz, x), c, pl.ds(0, R1))

            def buffer(k):
                return r1z.at[k, tz]

            def index(k):
                return k * 4 + tz

            if i < 3:
                along(tz, here, buffer, "r1z", index, extra)
            else:
                total = end(here, buffer, "r1z", index, extra)
                grad_o[pl.ds(0, R1)] = (total * scale).astype(BF)

        def r2z_step(i, g):
            tz = far[i]
            here = (tz, slice(None), (x + g) % 2, c, pl.ds(R1, R2))

            def buffer(k):
                return r2z.at[k, tz, g]

            def index(k):
                return (k * 4 + tz) * 2 + g

            if i < 3:
                along(tz, here, buffer, "r2z", index, [])
            else:
                d[here] = end(here, buffer, "r2z", index, []).astype(BF)

        def r2a():
            send(dr(z, xo, R1, R2H), r2h.at[0, pl.ds(0, R2H)], "r2h", 0, right)
            send(dr(z, xo, R1 + R2H, R2 - R2H), r2h.at[1, pl.ds(0, R2 - R2H)], "r2h", 1, left)

        def r2bL():
            got = r2h.at[0, pl.ds(0, R2H)]
            recv(got, "r2h", 0)
            add(z, xr, R1, R2H, got)
            send(dr(z, xr, R1, R2), r2f.at[0], "r2f", 0, right)

        def r2bR():
            got = r2h.at[1, pl.ds(0, R2 - R2H)]
            recv(got, "r2h", 1)
            add(z, xl, R1 + R2H, R2 - R2H, got)
            send(dr(z, xl, R1, R2), r2f.at[1], "r2f", 1, left)

        def r2c():
            recv(r2f.at[0], "r2f", 0)
            recv(r2f.at[1], "r2f", 1)
            total = d[(*chip(z, x), c, pl.ds(R1, R2))].astype(F32) + r2f[0].astype(F32) + r2f[1].astype(F32)
            grad_o[pl.ds(R1, R2)] = (total * scale).astype(BF)

        def outer_send():
            for copy in loads[3:]:
                copy.wait()
            for k in range(1, 4):
                ty = (y + k) % 4
                for h in range(2):
                    send(
                        fl.at[:, pl.ds(pl.multiple_of((h * 4 + ty) * COLS, COLS), COLS)],
                        ry.at[k - 1, h], "oy", (k - 1) * 2 + h, (zh * 4 + ty, me),
                    )
            moment_next = 0.9 * moment[...] + pending[...]
            anchor_next = anchor[...] - 0.7 * (pending[...] + 0.9 * moment_next)
            moment_o[...] = moment_next
            anchor_o[...] = anchor_next
            shared[zh, y] = anchor_next.astype(BF)
            send(shared.at[zh, y], shared.at[zh, y], "os", 0, other_zh)
            for k in range(1, 4):
                ty = (y + k) % 4
                send(shared.at[zh, y], shared.at[zh, y], "oy2", k - 1, (zh * 4 + ty, me))

        def outer_y():
            for k in range(1, 4):
                for h in range(2):
                    recv(ry.at[k - 1, h], "oy", (k - 1) * 2 + h)
            recv(shared.at[1 - zh, y], "os", 0)
            for k in range(1, 4):
                ty = (y + k) % 4
                send(shared.at[1 - zh, y], shared.at[1 - zh, y], "oy3", k - 1, (zh * 4 + ty, me))

            def local(h):
                total = fl[:, pl.ds(pl.multiple_of((h * 4 + y) * COLS, COLS), COLS)].astype(F32)
                for k in range(3):
                    total = total + ry[k, h].astype(F32)
                return total

            part_out[...] = local(1 - zh).astype(BF)
            send(part_out, part_in, "op", 0, other_zh)
            pending_o[...] = local(zh)

        def outer_mid():
            recv(part_in, "op", 0)
            pending_o[...] = anchor[...] - (pending_o[...] + part_in[...].astype(F32)) / 8

        def outer_end():
            for k in range(1, 4):
                ty = (y + 4 - k) % 4
                recv(shared.at[zh, ty], "oy2", k - 1)
                recv(shared.at[1 - zh, ty], "oy3", k - 1)
            for h in range(2):
                for q in range(4):
                    cols = pl.ds((h * 4 + q) * COLS, COLS)
                    local_o[:, cols] = (0.5 * fl[:, cols].astype(F32) + 0.5 * shared[h, q].astype(F32)).astype(BF)

        actions = {
            "o2x": o2x, "o1z": o1z, "g2": g2, "x1o": x1o, "z1": z1, "x1L": x1L, "x1R": x1R, "x1F": x1F, "a2L": a2L, "a2R": a2R, "a2F": a2F,
            "z2": z2, "sib": sib, "comp": comp, "dw": dw, "pair": pair, "r1a": r1a, "r1bL": r1bL, "r1bR": r1bR, "r1c": r1c,
            "r2z": r2z_step, "r2a": r2a, "r2bL": r2bL, "r2bR": r2bR, "r2c": r2c,
            "outer_send": outer_send, "outer_y": outer_y, "outer_mid": outer_mid, "outer_end": outer_end,
        }
        for name, *args in order:
            actions[name](*args)
        keys_o[...] = acc[...].astype(BF)
        for copy in pending_sends:
            copy.wait_send()

    pl.when(low | high)(functools.partial(body, False, order[0]))
    pl.when(jnp.logical_not(low | high))(functools.partial(body, True, order[1]))


def finish(*refs):
    sems = refs[-1]
    pairs = []
    for source, target in zip(refs[:7], refs[7:14], strict=True):
        parts = 4 if source.shape[1] == D else 1
        rows = source.shape[0] // parts
        pairs += [(source.at[pl.ds(k * rows, rows)], target.at[pl.ds(k * rows, rows)]) for k in range(parts)]
    copies = [pltpu.make_async_copy(s, t, sems.at[i]) for i, (s, t) in enumerate(pairs)]
    for copy in copies:
        copy.start()
    for copy in copies:
        copy.wait()


def launch(acts, key_weight, cotangent, frag_local, anchor, moment, pending, order=ORDER, A1=144, R1=144, name='window', cid=1):
    R2 = SH - R1
    R1H, R2H = R1 // 32 * 16, R2 // 32 * 16
    any_space = pl.BlockSpec(memory_space=pl.ANY)
    arrays = (acts[0], key_weight[0], cotangent[0], frag_local[0], anchor, moment, pending)
    vm = pltpu.VMEM
    outs = pl.pallas_call(
        functools.partial(kernel, order, A1, R1),
        out_shape=[
            vm((TOK, KW), BF), vm((SH, KW), BF), vm((TOK, D), BF), vm((SH, FW), BF),
            vm((SH, COLS), F32), vm((SH, COLS), F32), vm((SH, COLS), F32),
        ],
        in_specs=[any_space] * 7,
        out_specs=[pl.BlockSpec(memory_space=vm)] * 7,
        scratch_shapes=[
            vm((TOK, D), BF), vm((TOK, KW), BF), vm((SH, FW), BF),
            vm((SH, COLS), F32), vm((SH, COLS), F32), vm((SH, COLS), F32),
            vm((4, 2, 2, 2, SH, KW), BF), vm((4, 2, 2, 2, SH, KW), BF), vm((4, 2, 2, SH, KW), BF),
            vm((4, 2, max(R1H, R1 - R1H), KW), BF), vm((4, 2, R1, KW), BF), vm((2, 4, R1, KW), BF),
            vm((2, 4, 2, 2, R2, KW), BF), vm((2, max(R2H, R2 - R2H), KW), BF), vm((2, R2, KW), BF),
            vm((TOK, KW), F32), vm((3, 2, SH, COLS), BF), vm((2, 4, SH, COLS), BF), vm((SH, COLS), BF), vm((SH, COLS), BF),
            pltpu.SemaphoreType.DMA((TOTAL,)), pltpu.SemaphoreType.DMA((TOTAL,)),
            pltpu.SemaphoreType.DMA((LOADS,)),
        ],
        name=name,
        compiler_params=pltpu.CompilerParams(
            collective_id=cid, has_side_effects=True, vmem_limit_bytes=46 * 2**20
        ),
    )(*[pltpu.with_memory_space_constraint(a, pltpu.HBM) for a in arrays])
    outs = pl.pallas_call(
        finish,
        out_shape=[jax.ShapeDtypeStruct(o.shape, o.dtype) for o in outs],
        in_specs=[any_space] * 7,
        out_specs=[any_space] * 7,
        scratch_shapes=[pltpu.SemaphoreType.DMA((10,))],
        name="finish",
        compiler_params=pltpu.CompilerParams(vmem_limit_bytes=2**20),
    )(*[pltpu.with_memory_space_constraint(o, vm) for o in outs])
    keys, grad, back, local, anchor_next, moment_next, pending_next = outs
    return (keys[None], grad[None], back[None], local[None], anchor_next, moment_next, pending_next)


def on_device(*arrays):
    return launch(*arrays)


def solution(mesh):
    wide, flat = P("rep", "fsdp", None), P("fsdp", "rep")
    return jax.shard_map(
        on_device,
        mesh=mesh,
        in_specs=(wide,) * 4 + (flat,) * 3,
        out_specs=(wide,) * 4 + (flat,) * 3,
        check_vma=False,
    )
```

```python
import functools

import jax
import jax.numpy as jnp
from jax import lax
from jax.experimental import pallas as pl
from jax.experimental.pallas import tpu as pltpu
from jax.sharding import PartitionSpec as P

MESH = pl.DeviceIdType.MESH
BF = jnp.bfloat16
F32 = jnp.float32

TOK = 256
D = 7168
KW = 512
FW = 1024
SH = 224
CH = 896
COLS = 128
GROUP_TOKENS = 8192

COUNTS = (
    ("a1z", 8), ("a1x", 16), ("a2x", 4), ("a2z", 16), ("sib", 8), ("dp", 8),
    ("r1h", 8), ("r1f", 8), ("r1z", 8), ("r2z", 16), ("r2h", 2), ("r2f", 2),
    ("oy", 6), ("os", 1), ("oy2", 3), ("oy3", 3), ("op", 1),
)
BASE = {}
TOTAL = 0
for _name, _n in COUNTS:
    BASE[_name] = TOTAL
    TOTAL += _n
LOADS = 7
LAG = 40


ENDS = (
    ("o2x",), ("dw", 0), ("o1z",), ("x1o", 0), ("dw", 2), ("dw", 1), ("dw", 7), ("a2R",), ("dw", 3), ("pair", 1),
    ("pair", 0), ("a2L",), ("g2", 1), ("r1a", 0), ("pair", 2), ("pair", 7), ("dw", 6), ("pair", 3), ("x1R", 0),
    ("r2z", 0, 0), ("outer_send",), ("z1", 1), ("x1L", 0), ("x1o", 1), ("r2z", 1, 0), ("pair", 6), ("r1bR", 0),
    ("dw", 4), ("r1a", 1), ("a2F",), ("g2", 0), ("r2z", 1, 1), ("sib", 0, 0), ("z1", 2), ("r1bL", 0), ("x1F", 0),
    ("r2z", 0, 1), ("x1L", 1), ("dw", 5), ("r1bL", 1), ("pair", 5), ("x1o", 2), ("r1c", 0), ("z1", 3), ("x1o", 3),
    ("x1R", 1), ("pair", 4), ("x1R", 2), ("r2z", 2, 0), ("outer_y",), ("r2z", 2, 1), ("x1L", 2), ("r1bR", 1),
    ("outer_end",), ("x1L", 3), ("z2", 1, 1), ("x1F", 1), ("r1a", 2), ("comp", 0, 0), ("z2", 2, 0), ("x1R", 3),
    ("sib", 0, 1), ("z2", 2, 1), ("r1a", 3), ("sib", 2, 0), ("z2", 1, 0), ("x1F", 2), ("r1c", 1), ("r1bR", 2),
    ("r1bL", 2), ("sib", 2, 1), ("r2z", 3, 0), ("z2", 3, 1), ("sib", 1, 0), ("r2a",), ("x1F", 3), ("z2", 3, 0),
    ("r1bR", 3), ("r1bL", 3), ("comp", 2, 1), ("comp", 1, 0), ("sib", 3, 1), ("r2z", 3, 1), ("r2bL",), ("r1c", 2),
    ("comp", 0, 1), ("outer_mid",), ("sib", 3, 0), ("r2bR",), ("sib", 1, 1), ("comp", 3, 1), ("comp", 2, 0),
    ("comp", 3, 0), ("comp", 1, 1), ("r1c", 3), ("r2c",),
)
MIDDLE = (
    ("o2x",), ("dw", 0), ("x1o", 0), ("o1z",), ("dw", 4), ("outer_send",), ("a2L",), ("dw", 1), ("a2R",), ("g2", 1),
    ("pair", 4), ("pair", 0), ("z1", 1), ("r1a", 0), ("dw", 6), ("x1R", 0), ("z1", 2), ("x1o", 2), ("dw", 5),
    ("dw", 3), ("x1L", 0), ("a2F",), ("dw", 7), ("g2", 0), ("dw", 2), ("r1a", 2), ("pair", 3), ("pair", 1),
    ("z1", 3), ("pair", 5), ("sib", 0, 0), ("x1o", 1), ("x1o", 3), ("z2", 2, 1), ("pair", 2), ("pair", 7),
    ("r2z", 0, 0), ("r1a", 1), ("outer_y",), ("pair", 6), ("x1F", 0), ("z2", 1, 1), ("comp", 0, 0), ("x1R", 2),
    ("r1bL", 0), ("x1R", 1), ("z2", 2, 0), ("r1bR", 0), ("z2", 1, 0), ("x1L", 1), ("x1L", 3), ("z2", 3, 1),
    ("x1L", 2), ("r2z", 1, 0), ("x1F", 1), ("x1R", 3), ("r2z", 2, 0), ("r2z", 0, 1), ("r1bR", 1), ("sib", 1, 0),
    ("r1bL", 1), ("z2", 3, 0), ("r1a", 3), ("r2z", 1, 1), ("sib", 2, 0), ("r1bL", 2), ("sib", 1, 1), ("r1bR", 2),
    ("x1F", 2), ("r2z", 3, 0), ("sib", 2, 1), ("r1c", 0), ("comp", 1, 0), ("r2a",), ("r2z", 2, 1), ("r1bL", 3),
    ("comp", 1, 1), ("x1F", 3), ("comp", 2, 0), ("sib", 0, 1), ("r2z", 3, 1), ("r1bR", 3), ("r2bL",), ("sib", 3, 0),
    ("comp", 2, 1), ("sib", 3, 1), ("r1c", 2), ("r1c", 1), ("r2bR",), ("outer_mid",), ("outer_end",),
    ("comp", 3, 1), ("comp", 0, 1), ("comp", 3, 0), ("r1c", 3), ("r2c",),
)
ORDER = (ENDS, MIDDLE)


def kernel(
    order, A1, R1, acts_h, kw_h, cot_h, fl_h, anchor_h, moment_h, pending_h,
    keys_o, grad_o, back_o, local_o, anchor_o, moment_o, pending_o,
    acts, cot, fl, anchor, moment, pending,
    w, d, rb, r1h, r1f, r1z, r2z, r2h, r2f,
    acc, ry, shared, part_out, part_in,
    send_sem, recv_sem, load_sem,
):
    A2, R2 = SH - A1, SH - R1
    A1H, A2H, R1H, R2H = (n // 32 * 16 for n in (A1, A2, R1, R2))
    rep, me = lax.axis_index("rep"), lax.axis_index("fsdp")
    zh, y = rep // 4, rep % 4
    z, x, c = me // 8, (me // 2) % 4, me % 2
    xl, xr, xo = (x + 3) % 4, (x + 1) % 4, (x + 2) % 4
    at_z0, at_z1, at_z2, at_z3 = z == 0, z == 1, z == 2, z == 3
    low, high = z == 0, z == 3

    def table(a, b, e, f):
        return jnp.where(at_z0, a, jnp.where(at_z1, b, jnp.where(at_z2, e, f)))

    near = [z, table(1, 0, 3, 2), table(2, 2, 1, 1), table(3, 3, 0, 0)]
    far = near[::-1]

    def dev(tz, tx, tc):
        return (rep, tz * 8 + tx * 2 + tc)

    right, left = dev(z, xr, c), dev(z, xl, c)
    up, down = dev(jnp.minimum(z + 1, 3), x, c), dev(jnp.maximum(z - 1, 0), x, c)
    sibling = dev(z, x, 1 - c)
    other_zh = ((1 - zh) * 4 + y, me)

    def chip(tz, tx):
        return tz, tx // 2, tx % 2

    pending_sends = []

    def remote(src, dst, name, index, to):
        return pltpu.make_async_remote_copy(
            src_ref=src, dst_ref=dst,
            send_sem=send_sem.at[BASE[name] + index], recv_sem=recv_sem.at[BASE[name] + index],
            device_id=to, device_id_type=MESH,
        )

    def send(src, dst, name, index, to):
        copy = remote(src, dst, name, index, to)
        copy.start()
        pending_sends.append(copy)

    def recv(dst, name, index):
        remote(dst, dst, name, index, sibling).wait_recv()

    loads = [
        (kw_h, w.at[(*chip(z, x), c)]), (cot_h, cot), (acts_h, acts), (fl_h, fl),
        (anchor_h, anchor), (moment_h, moment), (pending_h, pending),
    ]
    loads = [pltpu.make_async_copy(s, t, load_sem.at[i]) for i, (s, t) in enumerate(loads)]
    for copy in loads:
        copy.start()

    barrier = pltpu.get_barrier_semaphore()

    def greet(to):
        pl.semaphore_signal(barrier, inc=1, device_id=to, device_id_type=MESH)

    for to in (left, right, sibling, other_zh):
        greet(to)
    for k in range(1, 4):
        greet((zh * 4 + (y + k) % 4, me))

    @pl.when(z < 3)
    def _():
        greet(up)

    @pl.when(z > 0)
    def _():
        greet(down)

    loads[0].wait()
    pl.semaphore_wait(barrier, 8 + jnp.where(low | high, 0, 1))

    inner = dev(jnp.where(low, 1, 2), x, c)

    def body(is_middle, order):
        def wr(tz, tx, start, size):
            return w.at[(*chip(tz, tx), c, pl.ds(start, size))]

        def a1_round(tz):
            for i, to in ((0, right), (1, left)):
                send(wr(tz, x, 0, A1), wr(tz, x, 0, A1), "a1x", tz * 4 + i, to)

        pending_sends.clear()
        tokens_here = []
        starts = ((0, up), (1, down)) if is_middle else ((jnp.where(low, 0, 1), inner),)

        def onward(tz):
            rising = tz < z
            return jnp.where(rising, 0, 1), dev(jnp.where(rising, z + 1, z - 1), x, c)

        def two(tz, g):
            return w.at[tz, :, (x + g) % 2, c, pl.ds(A1, A2)]

        def a2_along(tz, g, ways):
            for i, to in ways:
                send(two(tz, g), two(tz, g), "a2z", (i * 4 + tz) * 2 + g, to)

        def o2x():
            for i, to in ((0, right), (1, left)):
                send(wr(z, x, A1, A2), wr(z, x, A1, A2), "a2x", i, to)

        def o1z():
            for i, to in starts:
                send(wr(z, x, 0, A1), wr(z, x, 0, A1), "a1z", i * 4 + z, to)

        def g2(g):
            a2_along(z, g, starts)

        def x1o(j):
            a1_round(near[j])

        def z1(j):
            tz = near[j]
            rising = tz < z
            recv(wr(tz, x, 0, A1), "a1z", jnp.where(rising, 0, 4) + tz)
            if is_middle:
                piece = wr(tz, x, 0, A1)
                way, to = onward(tz)
                send(piece, piece, "a1z", way * 4 + tz, to)

        def x1L(j):
            tz = near[j]
            recv(wr(tz, xl, 0, A1), "a1x", tz * 4)
            piece = wr(tz, xl, 0, A1H)
            send(piece, piece, "a1x", tz * 4 + 2, right)

        def x1R(j):
            tz = near[j]
            recv(wr(tz, xr, 0, A1), "a1x", tz * 4 + 1)
            piece = wr(tz, xr, A1H, A1 - A1H)
            send(piece, piece, "a1x", tz * 4 + 3, left)

        def x1F(j):
            tz = near[j]
            recv(wr(tz, xo, 0, A1H), "a1x", tz * 4 + 2)
            recv(wr(tz, xo, A1H, A1 - A1H), "a1x", tz * 4 + 3)

        def a2L():
            recv(wr(z, xl, A1, A2), "a2x", 0)
            piece = wr(z, xl, A1, A2H)
            send(piece, piece, "a2x", 2, right)

        def a2R():
            recv(wr(z, xr, A1, A2), "a2x", 1)
            piece = wr(z, xr, A1 + A2H, A2 - A2H)
            send(piece, piece, "a2x", 3, left)

        def a2F():
            recv(wr(z, xo, A1, A2H), "a2x", 2)
            recv(wr(z, xo, A1 + A2H, A2 - A2H), "a2x", 3)

        def z2(j, g):
            tz = near[j]
            recv(two(tz, g), "a2z", (jnp.where(tz < z, 0, 4) + tz) * 2 + g)
            if is_middle:
                a2_along(tz, g, (onward(tz),))

        def half_of(j, p):
            tz, px = near[j], x // 2 if p == 0 else 1 - x // 2
            return tz * 2 + px, (tz, px)

        def sib(j, p):
            index, first = half_of(j, p)
            piece = w.at[(*first, slice(None), c)]
            send(piece, piece, "sib", index, sibling)

        def await_tokens():
            if not tokens_here:
                loads[1].wait()
                loads[2].wait()
                tokens_here.append(True)

        def comp(j, p):
            await_tokens()
            index, first = half_of(j, p)
            recv(w.at[(*first, slice(None), 1 - c)], "sib", index)
            col = pl.multiple_of(index * CH, CH)
            rows = w[first].reshape(CH, KW)
            got = jnp.dot(acts[:, pl.ds(col, CH)], rows, preferred_element_type=F32)
            if j == 0 and p == 0:
                acc[...] = got
            else:
                acc[...] += got
            back_o[:, pl.ds(col, CH)] = lax.dot_general(
                cot[...], rows, (((1,), (1,)), ((), ())), preferred_element_type=F32
            ).astype(BF)

        def grad_chunk(n):
            tz, px = far[n // 2], 1 - x // 2 if n % 2 == 0 else x // 2
            return tz * 2 + px, (tz, px)

        def dw(n):
            await_tokens()
            index, first = grad_chunk(n)
            col = pl.multiple_of(index * CH, CH)
            got = lax.dot_general(
                acts[:, pl.ds(col, CH)], cot[...], (((0,), (0,)), ((), ())), preferred_element_type=F32
            )
            d[first] = got.astype(BF).reshape(2, 2, SH, KW)
            send(d.at[(*first, slice(None), 1 - c)], rb.at[first], "dp", index, sibling)

        def pair(n):
            index, first = grad_chunk(n)
            recv(rb.at[first], "dp", index)
            for k in range(2):
                d[(*first, k, c)] = (d[(*first, k, c)].astype(F32) + rb[(*first, k)].astype(F32)).astype(BF)

        def add(tz, tx, start, size, *others):
            here = (*chip(tz, tx), c, pl.ds(start, size))
            total = d[here].astype(F32)
            for ref in others:
                total = total + ref[...].astype(F32)
            d[here] = total.astype(BF)

        def dr(tz, tx, start, size):
            return d.at[(*chip(tz, tx), c, pl.ds(start, size))]

        def r1a(i):
            tz = far[i]
            send(dr(tz, xo, 0, R1H), r1h.at[tz, 0, pl.ds(0, R1H)], "r1h", tz * 2, right)
            send(dr(tz, xo, R1H, R1 - R1H), r1h.at[tz, 1, pl.ds(0, R1 - R1H)], "r1h", tz * 2 + 1, left)

        def r1bL(i):
            tz = far[i]
            got = r1h.at[tz, 0, pl.ds(0, R1H)]
            recv(got, "r1h", tz * 2)
            add(tz, xr, 0, R1H, got)
            send(dr(tz, xr, 0, R1), r1f.at[tz, 0], "r1f", tz * 2, right)

        def r1bR(i):
            tz = far[i]
            got = r1h.at[tz, 1, pl.ds(0, R1 - R1H)]
            recv(got, "r1h", tz * 2 + 1)
            add(tz, xl, R1H, R1 - R1H, got)
            send(dr(tz, xl, 0, R1), r1f.at[tz, 1], "r1f", tz * 2 + 1, left)

        scale = GROUP_TOKENS ** -0.5

        def gather_up(here, others):
            total = d[here].astype(F32)
            for ref in others:
                total = total + ref[...].astype(F32)
            return total

        def along(tz, here, buffer, name, index, extra):
            rising = tz > z
            way = jnp.where(rising, 0, 1)
            got, where = buffer(way), index(way)
            if is_middle:
                recv(got, name, where)
                d[here] = gather_up(here, [got, *extra]).astype(BF)
            elif extra:
                d[here] = gather_up(here, extra).astype(BF)
            to = dev(jnp.where(rising, z + 1, z - 1), x, c)
            send(d.at[here], got, name, where, to)

        def end(here, buffer, name, index, extra):
            ways = (0, 1) if is_middle else (jnp.where(low, 1, 0),)
            for i in ways:
                recv(buffer(i), name, index(i))
            return gather_up(here, [buffer(i) for i in ways] + extra)

        def r1c(i):
            tz = far[i]
            recv(r1f.at[tz, 0], "r1f", tz * 2)
            recv(r1f.at[tz, 1], "r1f", tz * 2 + 1)
            extra = [r1f.at[tz, 0], r1f.at[tz, 1]]
            here = (*chip(tz, x), c, pl.ds(0, R1))

            def buffer(k):
                return r1z.at[k, tz]

            def index(k):
                return k * 4 + tz

            if i < 3:
                along(tz, here, buffer, "r1z", index, extra)
            else:
                total = end(here, buffer, "r1z", index, extra)
                grad_o[pl.ds(0, R1)] = (total * scale).astype(BF)

        def r2z_step(i, g):
            tz = far[i]
            here = (tz, slice(None), (x + g) % 2, c, pl.ds(R1, R2))

            def buffer(k):
                return r2z.at[k, tz, g]

            def index(k):
                return (k * 4 + tz) * 2 + g

            if i < 3:
                along(tz, here, buffer, "r2z", index, [])
            else:
                d[here] = end(here, buffer, "r2z", index, []).astype(BF)

        def r2a():
            send(dr(z, xo, R1, R2H), r2h.at[0, pl.ds(0, R2H)], "r2h", 0, right)
            send(dr(z, xo, R1 + R2H, R2 - R2H), r2h.at[1, pl.ds(0, R2 - R2H)], "r2h", 1, left)

        def r2bL():
            got = r2h.at[0, pl.ds(0, R2H)]
            recv(got, "r2h", 0)
            add(z, xr, R1, R2H, got)
            send(dr(z, xr, R1, R2), r2f.at[0], "r2f", 0, right)

        def r2bR():
            got = r2h.at[1, pl.ds(0, R2 - R2H)]
            recv(got, "r2h", 1)
            add(z, xl, R1 + R2H, R2 - R2H, got)
            send(dr(z, xl, R1, R2), r2f.at[1], "r2f", 1, left)

        def r2c():
            recv(r2f.at[0], "r2f", 0)
            recv(r2f.at[1], "r2f", 1)
            total = d[(*chip(z, x), c, pl.ds(R1, R2))].astype(F32) + r2f[0].astype(F32) + r2f[1].astype(F32)
            grad_o[pl.ds(R1, R2)] = (total * scale).astype(BF)

        def outer_send():
            for copy in loads[3:]:
                copy.wait()
            for k in range(1, 4):
                ty = (y + k) % 4
                for h in range(2):
                    send(
                        fl.at[:, pl.ds(pl.multiple_of((h * 4 + ty) * COLS, COLS), COLS)],
                        ry.at[k - 1, h], "oy", (k - 1) * 2 + h, (zh * 4 + ty, me),
                    )
            moment_next = 0.9 * moment[...] + pending[...]
            anchor_next = anchor[...] - 0.7 * (pending[...] + 0.9 * moment_next)
            moment_o[...] = moment_next
            anchor_o[...] = anchor_next
            shared[zh, y] = anchor_next.astype(BF)
            send(shared.at[zh, y], shared.at[zh, y], "os", 0, other_zh)
            for k in range(1, 4):
                ty = (y + k) % 4
                send(shared.at[zh, y], shared.at[zh, y], "oy2", k - 1, (zh * 4 + ty, me))

        def outer_y():
            for k in range(1, 4):
                for h in range(2):
                    recv(ry.at[k - 1, h], "oy", (k - 1) * 2 + h)
            recv(shared.at[1 - zh, y], "os", 0)
            for k in range(1, 4):
                ty = (y + k) % 4
                send(shared.at[1 - zh, y], shared.at[1 - zh, y], "oy3", k - 1, (zh * 4 + ty, me))

            def local(h):
                total = fl[:, pl.ds(pl.multiple_of((h * 4 + y) * COLS, COLS), COLS)].astype(F32)
                for k in range(3):
                    total = total + ry[k, h].astype(F32)
                return total

            part_out[...] = local(1 - zh).astype(BF)
            send(part_out, part_in, "op", 0, other_zh)
            pending_o[...] = local(zh)

        def outer_mid():
            recv(part_in, "op", 0)
            pending_o[...] = anchor[...] - (pending_o[...] + part_in[...].astype(F32)) / 8

        def outer_end():
            for k in range(1, 4):
                ty = (y + 4 - k) % 4
                recv(shared.at[zh, ty], "oy2", k - 1)
                recv(shared.at[1 - zh, ty], "oy3", k - 1)
            for h in range(2):
                for q in range(4):
                    cols = pl.ds((h * 4 + q) * COLS, COLS)
                    local_o[:, cols] = (0.5 * fl[:, cols].astype(F32) + 0.5 * shared[h, q].astype(F32)).astype(BF)

        actions = {
            "o2x": o2x, "o1z": o1z, "g2": g2, "x1o": x1o, "z1": z1, "x1L": x1L, "x1R": x1R, "x1F": x1F, "a2L": a2L, "a2R": a2R, "a2F": a2F,
            "z2": z2, "sib": sib, "comp": comp, "dw": dw, "pair": pair, "r1a": r1a, "r1bL": r1bL, "r1bR": r1bR, "r1c": r1c,
            "r2z": r2z_step, "r2a": r2a, "r2bL": r2bL, "r2bR": r2bR, "r2c": r2c,
            "outer_send": outer_send, "outer_y": outer_y, "outer_mid": outer_mid, "outer_end": outer_end,
        }
        issued, waited = [], 0
        for step, (name, *args) in enumerate(order):
            actions[name](*args)
            issued.append(len(pending_sends))
            if step >= LAG:
                for copy in pending_sends[waited:issued[step - LAG]]:
                    copy.wait_send()
                waited = issued[step - LAG]
        keys_o[...] = acc[...].astype(BF)
        for copy in pending_sends[waited:]:
            copy.wait_send()

    pl.when(low | high)(functools.partial(body, False, order[0]))
    pl.when(jnp.logical_not(low | high))(functools.partial(body, True, order[1]))


def finish(*refs):
    sems = refs[-1]
    pairs = []
    for source, target in zip(refs[:7], refs[7:14], strict=True):
        parts = 4 if source.shape[1] == D else 1
        rows = source.shape[0] // parts
        pairs += [(source.at[pl.ds(k * rows, rows)], target.at[pl.ds(k * rows, rows)]) for k in range(parts)]
    copies = [pltpu.make_async_copy(s, t, sems.at[i]) for i, (s, t) in enumerate(pairs)]
    for copy in copies:
        copy.start()
    for copy in copies:
        copy.wait()


def launch(acts, key_weight, cotangent, frag_local, anchor, moment, pending, order=ORDER, A1=144, R1=144, name='window', cid=1):
    R2 = SH - R1
    R1H, R2H = R1 // 32 * 16, R2 // 32 * 16
    any_space = pl.BlockSpec(memory_space=pl.ANY)
    arrays = (acts[0], key_weight[0], cotangent[0], frag_local[0], anchor, moment, pending)
    vm = pltpu.VMEM
    outs = pl.pallas_call(
        functools.partial(kernel, order, A1, R1),
        out_shape=[
            vm((TOK, KW), BF), vm((SH, KW), BF), vm((TOK, D), BF), vm((SH, FW), BF),
            vm((SH, COLS), F32), vm((SH, COLS), F32), vm((SH, COLS), F32),
        ],
        in_specs=[any_space] * 7,
        out_specs=[pl.BlockSpec(memory_space=vm)] * 7,
        scratch_shapes=[
            vm((TOK, D), BF), vm((TOK, KW), BF), vm((SH, FW), BF),
            vm((SH, COLS), F32), vm((SH, COLS), F32), vm((SH, COLS), F32),
            vm((4, 2, 2, 2, SH, KW), BF), vm((4, 2, 2, 2, SH, KW), BF), vm((4, 2, 2, SH, KW), BF),
            vm((4, 2, max(R1H, R1 - R1H), KW), BF), vm((4, 2, R1, KW), BF), vm((2, 4, R1, KW), BF),
            vm((2, 4, 2, 2, R2, KW), BF), vm((2, max(R2H, R2 - R2H), KW), BF), vm((2, R2, KW), BF),
            vm((TOK, KW), F32), vm((3, 2, SH, COLS), BF), vm((2, 4, SH, COLS), BF), vm((SH, COLS), BF), vm((SH, COLS), BF),
            pltpu.SemaphoreType.DMA((TOTAL,)), pltpu.SemaphoreType.DMA((TOTAL,)),
            pltpu.SemaphoreType.DMA((LOADS,)),
        ],
        name=name,
        compiler_params=pltpu.CompilerParams(
            collective_id=cid, has_side_effects=True, vmem_limit_bytes=46 * 2**20
        ),
    )(*[pltpu.with_memory_space_constraint(a, pltpu.HBM) for a in arrays])
    outs = pl.pallas_call(
        finish,
        out_shape=[jax.ShapeDtypeStruct(o.shape, o.dtype) for o in outs],
        in_specs=[any_space] * 7,
        out_specs=[any_space] * 7,
        scratch_shapes=[pltpu.SemaphoreType.DMA((10,))],
        name="finish",
        compiler_params=pltpu.CompilerParams(vmem_limit_bytes=2**20),
    )(*[pltpu.with_memory_space_constraint(o, vm) for o in outs])
    keys, grad, back, local, anchor_next, moment_next, pending_next = outs
    return (keys[None], grad[None], back[None], local[None], anchor_next, moment_next, pending_next)


def on_device(*arrays):
    return launch(*arrays)


def solution(mesh):
    wide, flat = P("rep", "fsdp", None), P("fsdp", "rep")
    return jax.shard_map(
        on_device,
        mesh=mesh,
        in_specs=(wide,) * 4 + (flat,) * 3,
        out_specs=(wide,) * 4 + (flat,) * 3,
        check_vma=False,
    )
```

```python
import functools

import jax
import jax.numpy as jnp
from jax import lax
from jax.experimental import pallas as pl
from jax.experimental.pallas import tpu as pltpu
from jax.sharding import PartitionSpec as P

MESH = pl.DeviceIdType.MESH
BF = jnp.bfloat16
F32 = jnp.float32

TOK = 256
D = 7168
KW = 512
FW = 1024
SH = 224
CH = 896
COLS = 128
GROUP_TOKENS = 8192

COUNTS = (
    ("a1z", 8), ("a1x", 16), ("a2x", 4), ("a2z", 16), ("sib", 8), ("dp", 8),
    ("r1h", 8), ("r1f", 8), ("r1z", 8), ("r2z", 16), ("r2h", 2), ("r2f", 2),
    ("oy", 6), ("os", 1), ("oy2", 3), ("oy3", 3), ("op", 1),
)
BASE = {}
TOTAL = 0
for _name, _n in COUNTS:
    BASE[_name] = TOTAL
    TOTAL += _n
LOADS = 10
QUARTER = TOK // 4
LAG = 40


ENDS = (
    ("o2x",), ("dw", 0), ("o1z",), ("x1o", 0), ("dw", 2), ("dw", 1), ("dw", 7), ("a2R",), ("dw", 3), ("pair", 1),
    ("pair", 0), ("a2L",), ("g2", 1), ("r1a", 0), ("pair", 2), ("pair", 7), ("dw", 6), ("pair", 3), ("x1R", 0),
    ("r2z", 0, 0), ("outer_send",), ("z1", 1), ("x1L", 0), ("x1o", 1), ("r2z", 1, 0), ("pair", 6), ("r1bR", 0),
    ("dw", 4), ("r1a", 1), ("a2F",), ("g2", 0), ("r2z", 1, 1), ("sib", 0, 0), ("z1", 2), ("r1bL", 0), ("x1F", 0),
    ("r2z", 0, 1), ("x1L", 1), ("dw", 5), ("r1bL", 1), ("pair", 5), ("x1o", 2), ("r1c", 0), ("z1", 3), ("x1o", 3),
    ("x1R", 1), ("pair", 4), ("x1R", 2), ("r2z", 2, 0), ("outer_y",), ("r2z", 2, 1), ("x1L", 2), ("r1bR", 1),
    ("outer_end",), ("x1L", 3), ("z2", 1, 1), ("x1F", 1), ("r1a", 2), ("comp", 0, 0), ("z2", 2, 0), ("x1R", 3),
    ("sib", 0, 1), ("z2", 2, 1), ("r1a", 3), ("sib", 2, 0), ("z2", 1, 0), ("x1F", 2), ("r1c", 1), ("r1bR", 2),
    ("r1bL", 2), ("sib", 2, 1), ("r2z", 3, 0), ("z2", 3, 1), ("sib", 1, 0), ("r2a",), ("x1F", 3), ("z2", 3, 0),
    ("r1bR", 3), ("r1bL", 3), ("comp", 2, 1), ("comp", 1, 0), ("sib", 3, 1), ("r2z", 3, 1), ("r2bL",), ("r1c", 2),
    ("comp", 0, 1), ("outer_mid",), ("sib", 3, 0), ("r2bR",), ("sib", 1, 1), ("comp", 3, 1), ("comp", 2, 0),
    ("comp", 3, 0), ("comp", 1, 1), ("r1c", 3), ("r2c",),
)
MIDDLE = (
    ("o2x",), ("dw", 0), ("x1o", 0), ("o1z",), ("dw", 4), ("outer_send",), ("a2L",), ("dw", 1), ("a2R",), ("g2", 1),
    ("pair", 4), ("pair", 0), ("z1", 1), ("r1a", 0), ("dw", 6), ("x1R", 0), ("z1", 2), ("x1o", 2), ("dw", 5),
    ("dw", 3), ("x1L", 0), ("a2F",), ("dw", 7), ("g2", 0), ("dw", 2), ("r1a", 2), ("pair", 3), ("pair", 1),
    ("z1", 3), ("pair", 5), ("sib", 0, 0), ("x1o", 1), ("x1o", 3), ("z2", 2, 1), ("pair", 2), ("pair", 7),
    ("r2z", 0, 0), ("r1a", 1), ("outer_y",), ("pair", 6), ("x1F", 0), ("z2", 1, 1), ("comp", 0, 0), ("x1R", 2),
    ("r1bL", 0), ("x1R", 1), ("z2", 2, 0), ("r1bR", 0), ("z2", 1, 0), ("x1L", 1), ("x1L", 3), ("z2", 3, 1),
    ("x1L", 2), ("r2z", 1, 0), ("x1F", 1), ("x1R", 3), ("r2z", 2, 0), ("r2z", 0, 1), ("r1bR", 1), ("sib", 1, 0),
    ("r1bL", 1), ("z2", 3, 0), ("r1a", 3), ("r2z", 1, 1), ("sib", 2, 0), ("r1bL", 2), ("sib", 1, 1), ("r1bR", 2),
    ("x1F", 2), ("r2z", 3, 0), ("sib", 2, 1), ("r1c", 0), ("comp", 1, 0), ("r2a",), ("r2z", 2, 1), ("r1bL", 3),
    ("comp", 1, 1), ("x1F", 3), ("comp", 2, 0), ("sib", 0, 1), ("r2z", 3, 1), ("r1bR", 3), ("r2bL",), ("sib", 3, 0),
    ("comp", 2, 1), ("sib", 3, 1), ("r1c", 2), ("r1c", 1), ("r2bR",), ("outer_mid",), ("outer_end",),
    ("comp", 3, 1), ("comp", 0, 1), ("comp", 3, 0), ("r1c", 3), ("r2c",),
)
ORDER = (ENDS, MIDDLE)


def kernel(
    order, A1, R1, acts_h, kw_h, cot_h, fl_h, anchor_h, moment_h, pending_h,
    keys_o, grad_o, back_o, local_o, anchor_o, moment_o, pending_o,
    acts, cot, fl, anchor, moment, pending,
    w, d, rb, r1h, r1f, r1z, r2z, r2h, r2f,
    acc, ry, shared, part_out, part_in,
    send_sem, recv_sem, load_sem,
):
    A2, R2 = SH - A1, SH - R1
    A1H, A2H, R1H, R2H = (n // 32 * 16 for n in (A1, A2, R1, R2))
    rep, me = lax.axis_index("rep"), lax.axis_index("fsdp")
    zh, y = rep // 4, rep % 4
    z, x, c = me // 8, (me // 2) % 4, me % 2
    xl, xr, xo = (x + 3) % 4, (x + 1) % 4, (x + 2) % 4
    at_z0, at_z1, at_z2, at_z3 = z == 0, z == 1, z == 2, z == 3
    low, high = z == 0, z == 3

    def table(a, b, e, f):
        return jnp.where(at_z0, a, jnp.where(at_z1, b, jnp.where(at_z2, e, f)))

    near = [z, table(1, 0, 3, 2), table(2, 2, 1, 1), table(3, 3, 0, 0)]
    far = near[::-1]

    def dev(tz, tx, tc):
        return (rep, tz * 8 + tx * 2 + tc)

    right, left = dev(z, xr, c), dev(z, xl, c)
    up, down = dev(jnp.minimum(z + 1, 3), x, c), dev(jnp.maximum(z - 1, 0), x, c)
    sibling = dev(z, x, 1 - c)
    other_zh = ((1 - zh) * 4 + y, me)

    def chip(tz, tx):
        return tz, tx // 2, tx % 2

    pending_sends = []

    def remote(src, dst, name, index, to):
        return pltpu.make_async_remote_copy(
            src_ref=src, dst_ref=dst,
            send_sem=send_sem.at[BASE[name] + index], recv_sem=recv_sem.at[BASE[name] + index],
            device_id=to, device_id_type=MESH,
        )

    def send(src, dst, name, index, to):
        copy = remote(src, dst, name, index, to)
        copy.start()
        pending_sends.append(copy)

    def recv(dst, name, index):
        remote(dst, dst, name, index, sibling).wait_recv()

    loads = [
        (kw_h, w.at[(*chip(z, x), c)]), (cot_h, cot),
        *[(acts_h.at[pl.ds(k * QUARTER, QUARTER)], acts.at[pl.ds(k * QUARTER, QUARTER)]) for k in range(4)],
        (fl_h, fl),
        (anchor_h, anchor), (moment_h, moment), (pending_h, pending),
    ]
    loads = [pltpu.make_async_copy(s, t, load_sem.at[i]) for i, (s, t) in enumerate(loads)]
    for copy in loads:
        copy.start()

    barrier = pltpu.get_barrier_semaphore()

    def greet(to):
        pl.semaphore_signal(barrier, inc=1, device_id=to, device_id_type=MESH)

    for to in (left, right, sibling, other_zh):
        greet(to)
    for k in range(1, 4):
        greet((zh * 4 + (y + k) % 4, me))

    @pl.when(z < 3)
    def _():
        greet(up)

    @pl.when(z > 0)
    def _():
        greet(down)

    loads[0].wait()
    pl.semaphore_wait(barrier, 8 + jnp.where(low | high, 0, 1))

    inner = dev(jnp.where(low, 1, 2), x, c)

    def body(is_middle, order):
        def wr(tz, tx, start, size):
            return w.at[(*chip(tz, tx), c, pl.ds(start, size))]

        def a1_round(tz):
            for i, to in ((0, right), (1, left)):
                send(wr(tz, x, 0, A1), wr(tz, x, 0, A1), "a1x", tz * 4 + i, to)

        pending_sends.clear()
        tokens_here = []
        starts = ((0, up), (1, down)) if is_middle else ((jnp.where(low, 0, 1), inner),)

        def onward(tz):
            rising = tz < z
            return jnp.where(rising, 0, 1), dev(jnp.where(rising, z + 1, z - 1), x, c)

        def two(tz, g):
            return w.at[tz, :, (x + g) % 2, c, pl.ds(A1, A2)]

        def a2_along(tz, g, ways):
            for i, to in ways:
                send(two(tz, g), two(tz, g), "a2z", (i * 4 + tz) * 2 + g, to)

        def o2x():
            for i, to in ((0, right), (1, left)):
                send(wr(z, x, A1, A2), wr(z, x, A1, A2), "a2x", i, to)

        def o1z():
            for i, to in starts:
                send(wr(z, x, 0, A1), wr(z, x, 0, A1), "a1z", i * 4 + z, to)

        def g2(g):
            a2_along(z, g, starts)

        def x1o(j):
            a1_round(near[j])

        def z1(j):
            tz = near[j]
            rising = tz < z
            recv(wr(tz, x, 0, A1), "a1z", jnp.where(rising, 0, 4) + tz)
            if is_middle:
                piece = wr(tz, x, 0, A1)
                way, to = onward(tz)
                send(piece, piece, "a1z", way * 4 + tz, to)

        def x1L(j):
            tz = near[j]
            recv(wr(tz, xl, 0, A1), "a1x", tz * 4)
            piece = wr(tz, xl, 0, A1H)
            send(piece, piece, "a1x", tz * 4 + 2, right)

        def x1R(j):
            tz = near[j]
            recv(wr(tz, xr, 0, A1), "a1x", tz * 4 + 1)
            piece = wr(tz, xr, A1H, A1 - A1H)
            send(piece, piece, "a1x", tz * 4 + 3, left)

        def x1F(j):
            tz = near[j]
            recv(wr(tz, xo, 0, A1H), "a1x", tz * 4 + 2)
            recv(wr(tz, xo, A1H, A1 - A1H), "a1x", tz * 4 + 3)

        def a2L():
            recv(wr(z, xl, A1, A2), "a2x", 0)
            piece = wr(z, xl, A1, A2H)
            send(piece, piece, "a2x", 2, right)

        def a2R():
            recv(wr(z, xr, A1, A2), "a2x", 1)
            piece = wr(z, xr, A1 + A2H, A2 - A2H)
            send(piece, piece, "a2x", 3, left)

        def a2F():
            recv(wr(z, xo, A1, A2H), "a2x", 2)
            recv(wr(z, xo, A1 + A2H, A2 - A2H), "a2x", 3)

        def z2(j, g):
            tz = near[j]
            recv(two(tz, g), "a2z", (jnp.where(tz < z, 0, 4) + tz) * 2 + g)
            if is_middle:
                a2_along(tz, g, (onward(tz),))

        def half_of(j, p):
            tz, px = near[j], x // 2 if p == 0 else 1 - x // 2
            return tz * 2 + px, (tz, px)

        def sib(j, p):
            index, first = half_of(j, p)
            piece = w.at[(*first, slice(None), c)]
            send(piece, piece, "sib", index, sibling)

        def await_tokens():
            if not tokens_here:
                for copy in loads[1:6]:
                    copy.wait()
                tokens_here.append(True)

        def comp(j, p):
            await_tokens()
            index, first = half_of(j, p)
            recv(w.at[(*first, slice(None), 1 - c)], "sib", index)
            col = pl.multiple_of(index * CH, CH)
            rows = w[first].reshape(CH, KW)
            got = jnp.dot(acts[:, pl.ds(col, CH)], rows, preferred_element_type=F32)
            if j == 0 and p == 0:
                acc[...] = got
            else:
                acc[...] += got
            back_o[:, pl.ds(col, CH)] = lax.dot_general(
                cot[...], rows, (((1,), (1,)), ((), ())), preferred_element_type=F32
            ).astype(BF)

        def grad_chunk(n):
            tz, px = far[n // 2], 1 - x // 2 if n % 2 == 0 else x // 2
            return tz * 2 + px, (tz, px)

        def dw(n):
            await_tokens()
            index, first = grad_chunk(n)
            col = pl.multiple_of(index * CH, CH)
            got = lax.dot_general(
                acts[:, pl.ds(col, CH)], cot[...], (((0,), (0,)), ((), ())), preferred_element_type=F32
            )
            d[first] = got.astype(BF).reshape(2, 2, SH, KW)
            send(d.at[(*first, slice(None), 1 - c)], rb.at[first], "dp", index, sibling)

        def pair(n):
            index, first = grad_chunk(n)
            recv(rb.at[first], "dp", index)
            for k in range(2):
                d[(*first, k, c)] = (d[(*first, k, c)].astype(F32) + rb[(*first, k)].astype(F32)).astype(BF)

        def add(tz, tx, start, size, *others):
            here = (*chip(tz, tx), c, pl.ds(start, size))
            total = d[here].astype(F32)
            for ref in others:
                total = total + ref[...].astype(F32)
            d[here] = total.astype(BF)

        def dr(tz, tx, start, size):
            return d.at[(*chip(tz, tx), c, pl.ds(start, size))]

        def r1a(i):
            tz = far[i]
            send(dr(tz, xo, 0, R1H), r1h.at[tz, 0, pl.ds(0, R1H)], "r1h", tz * 2, right)
            send(dr(tz, xo, R1H, R1 - R1H), r1h.at[tz, 1, pl.ds(0, R1 - R1H)], "r1h", tz * 2 + 1, left)

        def r1bL(i):
            tz = far[i]
            got = r1h.at[tz, 0, pl.ds(0, R1H)]
            recv(got, "r1h", tz * 2)
            add(tz, xr, 0, R1H, got)
            send(dr(tz, xr, 0, R1), r1f.at[tz, 0], "r1f", tz * 2, right)

        def r1bR(i):
            tz = far[i]
            got = r1h.at[tz, 1, pl.ds(0, R1 - R1H)]
            recv(got, "r1h", tz * 2 + 1)
            add(tz, xl, R1H, R1 - R1H, got)
            send(dr(tz, xl, 0, R1), r1f.at[tz, 1], "r1f", tz * 2 + 1, left)

        scale = GROUP_TOKENS ** -0.5

        def gather_up(here, others):
            total = d[here].astype(F32)
            for ref in others:
                total = total + ref[...].astype(F32)
            return total

        def along(tz, here, buffer, name, index, extra):
            rising = tz > z
            way = jnp.where(rising, 0, 1)
            got, where = buffer(way), index(way)
            if is_middle:
                recv(got, name, where)
                d[here] = gather_up(here, [got, *extra]).astype(BF)
            elif extra:
                d[here] = gather_up(here, extra).astype(BF)
            to = dev(jnp.where(rising, z + 1, z - 1), x, c)
            send(d.at[here], got, name, where, to)

        def end(here, buffer, name, index, extra):
            ways = (0, 1) if is_middle else (jnp.where(low, 1, 0),)
            for i in ways:
                recv(buffer(i), name, index(i))
            return gather_up(here, [buffer(i) for i in ways] + extra)

        def r1c(i):
            tz = far[i]
            recv(r1f.at[tz, 0], "r1f", tz * 2)
            recv(r1f.at[tz, 1], "r1f", tz * 2 + 1)
            extra = [r1f.at[tz, 0], r1f.at[tz, 1]]
            here = (*chip(tz, x), c, pl.ds(0, R1))

            def buffer(k):
                return r1z.at[k, tz]

            def index(k):
                return k * 4 + tz

            if i < 3:
                along(tz, here, buffer, "r1z", index, extra)
            else:
                total = end(here, buffer, "r1z", index, extra)
                grad_o[pl.ds(0, R1)] = (total * scale).astype(BF)

        def r2z_step(i, g):
            tz = far[i]
            here = (tz, slice(None), (x + g) % 2, c, pl.ds(R1, R2))

            def buffer(k):
                return r2z.at[k, tz, g]

            def index(k):
                return (k * 4 + tz) * 2 + g

            if i < 3:
                along(tz, here, buffer, "r2z", index, [])
            else:
                d[here] = end(here, buffer, "r2z", index, []).astype(BF)

        def r2a():
            send(dr(z, xo, R1, R2H), r2h.at[0, pl.ds(0, R2H)], "r2h", 0, right)
            send(dr(z, xo, R1 + R2H, R2 - R2H), r2h.at[1, pl.ds(0, R2 - R2H)], "r2h", 1, left)

        def r2bL():
            got = r2h.at[0, pl.ds(0, R2H)]
            recv(got, "r2h", 0)
            add(z, xr, R1, R2H, got)
            send(dr(z, xr, R1, R2), r2f.at[0], "r2f", 0, right)

        def r2bR():
            got = r2h.at[1, pl.ds(0, R2 - R2H)]
            recv(got, "r2h", 1)
            add(z, xl, R1 + R2H, R2 - R2H, got)
            send(dr(z, xl, R1, R2), r2f.at[1], "r2f", 1, left)

        def r2c():
            recv(r2f.at[0], "r2f", 0)
            recv(r2f.at[1], "r2f", 1)
            total = d[(*chip(z, x), c, pl.ds(R1, R2))].astype(F32) + r2f[0].astype(F32) + r2f[1].astype(F32)
            grad_o[pl.ds(R1, R2)] = (total * scale).astype(BF)

        def outer_send():
            for copy in loads[6:]:
                copy.wait()
            for k in range(1, 4):
                ty = (y + k) % 4
                for h in range(2):
                    send(
                        fl.at[:, pl.ds(pl.multiple_of((h * 4 + ty) * COLS, COLS), COLS)],
                        ry.at[k - 1, h], "oy", (k - 1) * 2 + h, (zh * 4 + ty, me),
                    )
            moment_next = 0.9 * moment[...] + pending[...]
            anchor_next = anchor[...] - 0.7 * (pending[...] + 0.9 * moment_next)
            moment_o[...] = moment_next
            anchor_o[...] = anchor_next
            shared[zh, y] = anchor_next.astype(BF)
            send(shared.at[zh, y], shared.at[zh, y], "os", 0, other_zh)
            for k in range(1, 4):
                ty = (y + k) % 4
                send(shared.at[zh, y], shared.at[zh, y], "oy2", k - 1, (zh * 4 + ty, me))

        def outer_y():
            for k in range(1, 4):
                for h in range(2):
                    recv(ry.at[k - 1, h], "oy", (k - 1) * 2 + h)
            recv(shared.at[1 - zh, y], "os", 0)
            for k in range(1, 4):
                ty = (y + k) % 4
                send(shared.at[1 - zh, y], shared.at[1 - zh, y], "oy3", k - 1, (zh * 4 + ty, me))

            def local(h):
                total = fl[:, pl.ds(pl.multiple_of((h * 4 + y) * COLS, COLS), COLS)].astype(F32)
                for k in range(3):
                    total = total + ry[k, h].astype(F32)
                return total

            part_out[...] = local(1 - zh).astype(BF)
            send(part_out, part_in, "op", 0, other_zh)
            pending_o[...] = local(zh)

        def outer_mid():
            recv(part_in, "op", 0)
            pending_o[...] = anchor[...] - (pending_o[...] + part_in[...].astype(F32)) / 8

        def outer_end():
            for k in range(1, 4):
                ty = (y + 4 - k) % 4
                recv(shared.at[zh, ty], "oy2", k - 1)
                recv(shared.at[1 - zh, ty], "oy3", k - 1)
            for h in range(2):
                for q in range(4):
                    cols = pl.ds((h * 4 + q) * COLS, COLS)
                    local_o[:, cols] = (0.5 * fl[:, cols].astype(F32) + 0.5 * shared[h, q].astype(F32)).astype(BF)

        actions = {
            "o2x": o2x, "o1z": o1z, "g2": g2, "x1o": x1o, "z1": z1, "x1L": x1L, "x1R": x1R, "x1F": x1F, "a2L": a2L, "a2R": a2R, "a2F": a2F,
            "z2": z2, "sib": sib, "comp": comp, "dw": dw, "pair": pair, "r1a": r1a, "r1bL": r1bL, "r1bR": r1bR, "r1c": r1c,
            "r2z": r2z_step, "r2a": r2a, "r2bL": r2bL, "r2bR": r2bR, "r2c": r2c,
            "outer_send": outer_send, "outer_y": outer_y, "outer_mid": outer_mid, "outer_end": outer_end,
        }
        issued, waited = [], 0
        for step, (name, *args) in enumerate(order):
            actions[name](*args)
            issued.append(len(pending_sends))
            if step >= LAG:
                for copy in pending_sends[waited:issued[step - LAG]]:
                    copy.wait_send()
                waited = issued[step - LAG]
        keys_o[...] = acc[...].astype(BF)
        for copy in pending_sends[waited:]:
            copy.wait_send()

    pl.when(low | high)(functools.partial(body, False, order[0]))
    pl.when(jnp.logical_not(low | high))(functools.partial(body, True, order[1]))


def finish(*refs):
    sems = refs[-1]
    pairs = []
    for source, target in zip(refs[:7], refs[7:14], strict=True):
        parts = 4 if source.shape[1] == D else 1
        rows = source.shape[0] // parts
        pairs += [(source.at[pl.ds(k * rows, rows)], target.at[pl.ds(k * rows, rows)]) for k in range(parts)]
    copies = [pltpu.make_async_copy(s, t, sems.at[i]) for i, (s, t) in enumerate(pairs)]
    for copy in copies:
        copy.start()
    for copy in copies:
        copy.wait()


def launch(acts, key_weight, cotangent, frag_local, anchor, moment, pending, order=ORDER, A1=144, R1=144, name='window', cid=1):
    R2 = SH - R1
    R1H, R2H = R1 // 32 * 16, R2 // 32 * 16
    any_space = pl.BlockSpec(memory_space=pl.ANY)
    arrays = (acts[0], key_weight[0], cotangent[0], frag_local[0], anchor, moment, pending)
    vm = pltpu.VMEM
    outs = pl.pallas_call(
        functools.partial(kernel, order, A1, R1),
        out_shape=[
            vm((TOK, KW), BF), vm((SH, KW), BF), vm((TOK, D), BF), vm((SH, FW), BF),
            vm((SH, COLS), F32), vm((SH, COLS), F32), vm((SH, COLS), F32),
        ],
        in_specs=[any_space] * 7,
        out_specs=[pl.BlockSpec(memory_space=vm)] * 7,
        scratch_shapes=[
            vm((TOK, D), BF), vm((TOK, KW), BF), vm((SH, FW), BF),
            vm((SH, COLS), F32), vm((SH, COLS), F32), vm((SH, COLS), F32),
            vm((4, 2, 2, 2, SH, KW), BF), vm((4, 2, 2, 2, SH, KW), BF), vm((4, 2, 2, SH, KW), BF),
            vm((4, 2, max(R1H, R1 - R1H), KW), BF), vm((4, 2, R1, KW), BF), vm((2, 4, R1, KW), BF),
            vm((2, 4, 2, 2, R2, KW), BF), vm((2, max(R2H, R2 - R2H), KW), BF), vm((2, R2, KW), BF),
            vm((TOK, KW), F32), vm((3, 2, SH, COLS), BF), vm((2, 4, SH, COLS), BF), vm((SH, COLS), BF), vm((SH, COLS), BF),
            pltpu.SemaphoreType.DMA((TOTAL,)), pltpu.SemaphoreType.DMA((TOTAL,)),
            pltpu.SemaphoreType.DMA((LOADS,)),
        ],
        name=name,
        compiler_params=pltpu.CompilerParams(
            collective_id=cid, has_side_effects=True, vmem_limit_bytes=46 * 2**20
        ),
    )(*[pltpu.with_memory_space_constraint(a, pltpu.HBM) for a in arrays])
    outs = pl.pallas_call(
        finish,
        out_shape=[jax.ShapeDtypeStruct(o.shape, o.dtype) for o in outs],
        in_specs=[any_space] * 7,
        out_specs=[any_space] * 7,
        scratch_shapes=[pltpu.SemaphoreType.DMA((10,))],
        name="finish",
        compiler_params=pltpu.CompilerParams(vmem_limit_bytes=2**20),
    )(*[pltpu.with_memory_space_constraint(o, vm) for o in outs])
    keys, grad, back, local, anchor_next, moment_next, pending_next = outs
    return (keys[None], grad[None], back[None], local[None], anchor_next, moment_next, pending_next)


def on_device(*arrays):
    return launch(*arrays)


def solution(mesh):
    wide, flat = P("rep", "fsdp", None), P("fsdp", "rep")
    return jax.shard_map(
        on_device,
        mesh=mesh,
        in_specs=(wide,) * 4 + (flat,) * 3,
        out_specs=(wide,) * 4 + (flat,) * 3,
        check_vma=False,
    )
```
